128 devices in a mesh: req: 8 (over z, core), cache: 16 (over y, x).
Axes of the slice: x: 4, y: 4, z: 4, core: 2. Of those that a mesh axis runs over, the one named last changes fastest.
Arguments:
- event_feats: bfloat16 [128, 512, 1024], P(('req', 'cache')), may hold values from -6 to 6
- hist_len: int32 [128, 16], P(('req', 'cache')), may hold values from 1 to 64, 512 in all within a row
- user_owner: int32 [128, 16], P(('req', 'cache')), may hold values from 0 to 15, each once within a row
- cand_ids: int32 [128, 1024], P(('req', 'cache')), may hold values from 0 to 1023
- cand_count: int32 [128, 8], P(('req', 'cache')), may hold values from 1 to 128, 512 in all within a row
- req_owner: int32 [128, 8], P(('req', 'cache')), may hold values from 0 to 7, each once within a row
- req_slot: int32 [128, 8], P(('req', 'cache')), may hold values from 0 to 15
- table: bfloat16 [1024, 1024], replicated, may hold values from -6 to 6
- w_qu: bfloat16 [1024, 2048], replicated, may hold values from -0.1875 to 0.1875
- w_kv: bfloat16 [1024, 2048], replicated, may hold values from -0.1875 to 0.1875
- w_out: bfloat16 [1024, 1024], replicated, may hold values from -0.1875 to 0.1875
Outputs:
- cache_kv: bfloat16 [128, 16, 64, 2048], P(('req', 'cache'))
- cand_out: bfloat16 [128, 1024, 1024], P(('req', 'cache'))
The draws below stay inside these ranges and needn't reach their ends.
Inputs may be any that keep to these rules, and one draw needn't show every extreme that they name: `hist_len`: each device's users together hold exactly 512 events. `user_owner`: each row names every index along cache once. `req_owner`: each row names every index along req once.
All inputs are finite; a program needn't handle non-finite values.
Results may differ from the reference program's by a relative error of at most 0.0063.
Values may be sent and summed in bfloat16 or wider, within the bound.
A program may use at most 128 MiB of HBM per device.

```python
import math
import jax
import jax.numpy as jnp
import numpy as np
from jax import lax

D = 1024
HEADS = 8
HEAD_DIM = 128
VOCAB = 1024
HIST = 64
CB = 128
U_DEV = 16
R_DEV = 8
PRE_ROWS = 512
N_REQ = 8
N_CACHE = 16
DEVICES = 128


def touch_ends(drawn, stream_key, smallest, largest):
    index_at = [jax.random.randint(jax.random.fold_in(stream_key, axis), (), 0, length) for axis, length in enumerate(drawn.shape)]
    widest = drawn.shape.index(max(drawn.shape))
    neighbour = index_at[:widest] + [(index_at[widest] + 1) % drawn.shape[widest]] + index_at[widest + 1:]
    return drawn.at[tuple(index_at)].set(smallest).at[tuple(neighbour)].set(largest)


def shard_levels(key, shape, shards, least, top_value):
    def one(dim, blocks):
        heights = jax.random.uniform(jax.random.fold_in(jax.random.fold_in(key, 6), dim), (blocks,), jnp.float32, least / len(shards), top_value / len(shards))
        return jnp.repeat(jnp.exp(heights), shape[dim] // blocks).reshape((-1,) + (1,) * (len(shape) - dim - 1))

    factor_of = one(*shards[0])
    for cut in shards[1:]:
        factor_of = factor_of * one(*cut)
    return factor_of


def profile(amount, total, most, slope):
    weights = [(1 << 20) // math.isqrt(grade ** slope) + 1 for grade in range(2, amount + 1)]
    spare, holding = total - most - (amount - 1), [1] * (amount - 1)
    while spare > 0:
        free = [i for i in range(amount - 1) if holding[i] < most]
        whole, remaining = sum([weights[i] for i in free]), spare
        for i in free:
            more = min(most - holding[i], max(1, remaining * weights[i] // whole), spare)
            holding[i] = holding[i] + more
            spare = spare - more
    return np.array([most] + holding)


def ragged_sizes(key, number_of, total, reach, slope):
    if number_of == 2:
        one = jax.random.randint(key, (), max(1, total - reach), min(reach, total - 1) + 1)
        return jnp.stack([one, total - one])
    lengths = jnp.asarray(profile(number_of, total, reach, slope), jnp.int32)
    pairs = (number_of - 1) // 2
    donor, taker = lengths[1:1 + 2 * pairs:2], lengths[2:2 + 2 * pairs:2]
    room = jnp.minimum(donor - 1, reach - taker)
    passed = jax.random.randint(jax.random.fold_in(key, 1), (pairs,), 0, 1 << 20) % (room + 1)
    lengths = lengths.at[1:1 + 2 * pairs:2].set(donor - passed).at[2:2 + 2 * pairs:2].set(taker + passed)
    return lengths[jax.random.permutation(jax.random.fold_in(key, 2), number_of)]


def bell_draw(key, dims, width, bound, cuts=(), kind=jnp.bfloat16):
    values = jax.random.normal(key, dims, jnp.float32) * width
    if len(cuts) > 0:
        values = shard_levels(key, dims, cuts, -0.22, 0.18) * values
    return jnp.clip(values, min=-bound, max=bound).astype(kind)


def setup_inputs(seed: int = 0) -> dict:
    arg_keys = jax.random.split(jax.random.key(seed), 12)
    event_feats = bell_draw(arg_keys[0], (DEVICES, PRE_ROWS, D), 1.0, 6.0, ((0, 128),))
    hist_len = jax.vmap(lambda own: ragged_sizes(own, U_DEV, PRE_ROWS, HIST, 2))(jax.random.split(arg_keys[1], DEVICES)).reshape((DEVICES, U_DEV)).astype(jnp.int32)
    user_owner = jax.vmap(lambda own: jax.random.permutation(own, N_CACHE))(jax.random.split(arg_keys[2], DEVICES)).reshape((DEVICES, U_DEV)).astype(jnp.int32)
    cand_ids = touch_ends(jax.random.randint(arg_keys[3], (DEVICES, R_DEV * CB), 0, VOCAB), jax.random.fold_in(arg_keys[3], 1), 0, VOCAB - 1).astype(jnp.int32)
    cand_count = jax.vmap(lambda own: ragged_sizes(own, R_DEV, R_DEV * CB // 2, CB, 2))(jax.random.split(arg_keys[4], DEVICES)).reshape((DEVICES, R_DEV)).astype(jnp.int32)
    req_owner = jax.vmap(lambda own: jax.random.permutation(own, N_REQ))(jax.random.split(arg_keys[5], DEVICES)).reshape((DEVICES, R_DEV)).astype(jnp.int32)
    req_slot = touch_ends(jax.random.randint(arg_keys[6], (DEVICES, R_DEV), 0, N_CACHE), jax.random.fold_in(arg_keys[6], 1), 0, N_CACHE - 1).astype(jnp.int32)
    table = bell_draw(arg_keys[7], (VOCAB, D), 1.0, 6.0)
    w_qu = bell_draw(arg_keys[8], (D, 2 * D), D ** -0.5, 0.1875)
    w_kv = bell_draw(arg_keys[9], (D, 2 * D), D ** -0.5, 0.1875)
    w_out = bell_draw(arg_keys[10], (D, D), D ** -0.5, 0.1875)
    return {"event_feats": event_feats, "hist_len": hist_len, "user_owner": user_owner, "cand_ids": cand_ids, "cand_count": cand_count, "req_owner": req_owner, "req_slot": req_slot, "table": table, "w_qu": w_qu, "w_kv": w_kv, "w_out": w_out}


def layer_norm(values):
    mean = lax.optimization_barrier(jnp.mean(values, axis=-1, keepdims=True))
    centred = values - mean
    spread = lax.optimization_barrier(jnp.mean(centred * centred, axis=-1, keepdims=True))
    return centred * lax.rsqrt(spread + 1e-06)

def embed_rows(row_ids, table):
    embedded = jnp.take(table, row_ids, axis=0)
    normed = layer_norm(embedded.astype(jnp.float32)).astype(jnp.bfloat16)
    return (embedded, normed)

def silu_proj(normed, weight):
    return jax.nn.silu(jnp.dot(normed, weight, preferred_element_type=jnp.float32)).astype(jnp.bfloat16)

def history_attend(queries, blocks):
    block_count = queries.shape[0]
    block_rows = queries.shape[1]
    query_heads = queries.reshape(block_count, block_rows, HEADS, HEAD_DIM).astype(jnp.float32)
    key_heads = blocks[:, :, :D].reshape(block_count, HIST, HEADS, HEAD_DIM).astype(jnp.float32)
    value_heads = blocks[:, :, D:].reshape(block_count, HIST, HEADS, HEAD_DIM).astype(jnp.float32)
    scores = jnp.einsum('rihd,rthd->rhit', query_heads, key_heads) * HEAD_DIM ** (-0.5)
    weights = jax.nn.silu(scores).astype(jnp.bfloat16)
    mixed = jnp.einsum('rhit,rthd->rihd', weights.astype(jnp.float32), value_heads)
    return mixed.reshape(block_count, block_rows, D).astype(jnp.bfloat16)

def finish(embedded, query_gate, keys_vals, hist_att, counts, w_out):
    query_heads = query_gate[:, :D].astype(jnp.float32).reshape(-1, HEADS, HEAD_DIM)
    key_heads = keys_vals[:, :D].astype(jnp.float32).reshape(-1, HEADS, HEAD_DIM)
    value_heads = keys_vals[:, D:].astype(jnp.float32).reshape(-1, HEADS, HEAD_DIM)
    self_weight = jax.nn.silu(lax.optimization_barrier(jnp.sum(query_heads * key_heads, axis=-1)) * HEAD_DIM ** (-0.5))
    self_term = (self_weight[..., None] * value_heads).reshape(-1, D)
    attended = hist_att.astype(jnp.float32) + self_term
    gated = (layer_norm(attended) * query_gate[:, D:].astype(jnp.float32)).astype(jnp.bfloat16)
    result = jnp.dot(gated, w_out, preferred_element_type=jnp.float32) + embedded.astype(jnp.float32)
    slot_ids = jnp.arange(result.shape[0], dtype=jnp.int32)
    live_rows = slot_ids % CB < counts[slot_ids // CB]
    return jnp.where(live_rows[:, None], result, jnp.zeros_like(result)).astype(jnp.bfloat16)

def reference(event_feats, hist_len, user_owner, cand_ids, cand_count, req_owner, req_slot, table, w_qu, w_kv, w_out):

    def prefill(feats):
        normed = layer_norm(feats.astype(jnp.float32)).astype(jnp.bfloat16)
        return silu_proj(normed, w_kv)
    hist_kv = lax.map(prefill, event_feats)
    starts = jnp.cumsum(hist_len, axis=1) - hist_len
    positions = jnp.arange(HIST, dtype=jnp.int32)

    def build(owner_dev):
        row_base = owner_dev // N_CACHE * N_CACHE
        column = owner_dev % N_CACHE
        sources = row_base + jnp.arange(N_CACHE, dtype=jnp.int32)
        picked = jnp.argmax(user_owner[sources] == column, axis=1).astype(jnp.int32)
        first_row = starts[sources, picked]
        length = hist_len[sources, picked]
        row_index = jnp.clip(first_row[:, None] + positions[None, :], 0, PRE_ROWS - 1).astype(jnp.int32)
        gathered = hist_kv[sources[:, None], row_index]
        live_mask = (positions[None, :] < length[:, None])[..., None]
        return jnp.where(live_mask, gathered, jnp.zeros_like(gathered))
    cache_kv = lax.map(build, jnp.arange(DEVICES, dtype=jnp.int32))

    def score(device):
        embedded, normed = embed_rows(cand_ids[device], table)
        query_gate = silu_proj(normed, w_qu)
        keys_vals = silu_proj(normed, w_kv)
        owner_dev = req_owner[device] * N_CACHE + device % N_CACHE
        blocks = cache_kv[owner_dev, req_slot[device]]
        queries = query_gate[:, :D].reshape(R_DEV, CB, D)
        hist_att = history_attend(queries, blocks).reshape(R_DEV * CB, D)
        return finish(embedded, query_gate, keys_vals, hist_att, cand_count[device], w_out)
    cand_out = lax.map(score, jnp.arange(DEVICES, dtype=jnp.int32))
    return (cache_kv, cand_out)
```

```python
import jax
import jax.numpy as jnp
from jax import lax
from jax.experimental import pallas as pl
from jax.experimental.pallas import tpu as pltpu
from jax.sharding import PartitionSpec as P

D = 1024
HEADS = 8
HEAD_DIM = 128
HIST = 64
CB = 128
USERS = 16
REQS = 8
ROWS = 512
LIVE = 512
CHUNK = 16
CHUNKS = HIST // CHUNK
SCALE = HEAD_DIM ** (-0.5)
MESH = pl.DeviceIdType.MESH
F32 = jnp.float32
BF16 = jnp.bfloat16
I32 = jnp.int32

XY = [(2, 2), (0, 2), (2, 0), (3, 1), (1, 3), (3, 3), (1, 1), (2, 3), (3, 2), (2, 1), (1, 2), (3, 0), (0, 3), (1, 0), (0, 1)]
ZK = [(2, 0), (2, 1), (1, 0), (3, 0), (1, 1), (3, 1), (0, 1)]


def iota(shape, dim):
    return lax.broadcasted_iota(I32, shape, dim)


def silu(x):
    half = 0.5 * x
    return half + half * jnp.tanh(half)


def norm(x):
    mean = jnp.sum(x, axis=-1, keepdims=True) * (1.0 / D)
    centred = x - mean
    spread = jnp.sum(centred * centred, axis=-1, keepdims=True) * (1.0 / D)
    return centred * lax.rsqrt(spread + 1e-06)


def dot(a, b):
    return jnp.dot(a, b, preferred_element_type=F32)


def dot_nt(a, b):
    return lax.dot_general(a, b, (((1,), (1,)), ((), ())), preferred_element_type=F32)


def loop(n, body):
    def step(i, carry):
        body(i)
        return carry

    lax.fori_loop(0, n, step, 0)


def cols(i, width):
    return pl.ds(pl.multiple_of(i * width, width), width)


def request_bounds(counts):
    lane = iota((1, REQS), 1)
    starts = [jnp.sum(jnp.where(lane < j, counts, 0.0), axis=1, keepdims=True) for j in range(REQS)]
    lengths = [jnp.sum(jnp.where(lane == j, counts, 0.0), axis=1, keepdims=True) for j in range(REQS)]
    return starts, lengths


def exchange_kernel(
    feats_h, len_h, own_h, ids_h, count_h, rown_h, rslot_h, table_h, wqu_h, wkv_h,
    cache_h, gated_h, emb_h,
    feats, len_v, own_v, ids_v, count_v, rown_v, rslot_v, table, wqu, wkv,
    hn, pick, send, recv0, recv1, recv2, recv3, slot_out, slot_in, select,
    stage, back0, back1, back2, back3, kv, kvr,
    onehot, emb, cn, query, gate, skv, att, mask, gated,
    load_sem, ss1, rs1, ss2, rs2, sss, rss, out_sem, emb_sem, gated_sem,
):
    r = lax.axis_index("req")
    c = lax.axis_index("cache")
    z, k = r // 2, lax.rem(r, 2)
    y, x = c // 4, lax.rem(c, 4)
    recv = [recv0, recv1, recv2, recv3]
    back = [back0, back1, back2, back3]

    def plane(offset):
        dy, dx = offset
        return lax.rem(y + dy, 4) * 4 + lax.rem(x + dx, 4)

    def column(offset):
        dz, dk = offset
        return lax.rem(z + dz, 4) * 2 + lax.rem(k + dk, 2)

    barrier = pltpu.get_barrier_semaphore()
    for offset in XY:
        pl.semaphore_signal(barrier, inc=1, device_id=(r, plane(offset)), device_id_type=MESH)
    for offset in ZK:
        pl.semaphore_signal(barrier, inc=1, device_id=(column(offset), c), device_id_type=MESH)

    pairs = [
        (len_h, len_v), (own_h, own_v), (feats_h, feats), (count_h, count_v), (ids_h, ids_v), (rown_h, rown_v), (rslot_h, rslot_v),
        (table_h, table), (wqu_h, wqu), (wkv_h, wkv),
    ]
    loads = [pltpu.make_async_copy(src, dst, load_sem.at[i]) for i, (src, dst) in enumerate(pairs)]
    for copy in loads:
        copy.start()

    loads[0].wait()
    loads[1].wait()
    lengths = len_v[...].astype(F32)
    owner = own_v[...]
    lane_j = iota((USERS, USERS), 1)
    mine = owner == iota((USERS, USERS), 0)
    order = jnp.sum(jnp.where(mine, lane_j.astype(F32), 0.0), axis=1, keepdims=True)
    length_of = jnp.sum(jnp.where(mine, lengths, 0.0), axis=1, keepdims=True)
    start_of = jnp.sum(jnp.where(lane_j.astype(F32) < order, lengths, 0.0), axis=1, keepdims=True)
    row = iota((CHUNK, ROWS), 1).astype(F32)
    step_t = iota((CHUNK, ROWS), 0).astype(F32)
    for o in range(USERS):
        place = row - start_of[o : o + 1, :]
        live = place < length_of[o : o + 1, :]
        for q in range(CHUNKS):
            hit = jnp.logical_and(place == step_t + float(q * CHUNK), live)
            pick[q, o * CHUNK : (o + 1) * CHUNK, :] = jnp.where(hit, 1.0, 0.0).astype(BF16)

    loads[2].wait()

    def norm_feats(i):
        rows = cols(i, 64)
        hn[rows, :] = norm(feats[rows, :].astype(F32)).astype(BF16)

    loop(ROWS // 64, norm_feats)

    def slot_copy(i):
        to = column(ZK[i])
        return pltpu.make_async_remote_copy(
            src_ref=slot_out.at[to], dst_ref=slot_in.at[r], send_sem=sss.at[i], recv_sem=rss.at[i],
            device_id=(to, c), device_id_type=MESH,
        )

    def plane_copy(q, i):
        to = plane(XY[i])
        return pltpu.make_async_remote_copy(
            src_ref=send.at[q, cols(to, CHUNK), :], dst_ref=recv[q].at[cols(c, CHUNK), :],
            send_sem=ss1.at[q, i], recv_sem=rs1.at[q, i], device_id=(r, to), device_id_type=MESH,
        )

    def column_copy(q, i):
        to = column(ZK[i])
        return pltpu.make_async_remote_copy(
            src_ref=stage.at[q, cols(to, CHUNK), :], dst_ref=back[q].at[cols(r, CHUNK), :],
            send_sem=ss2.at[q, i], recv_sem=rs2.at[q, i], device_id=(to, c), device_id_type=MESH,
        )

    for q in range(CHUNKS):
        for n in range(2):
            send[q, :, n * 512 : (n + 1) * 512] = dot(pick[q], hn[:, n * 512 : (n + 1) * 512]).astype(BF16)
        if q == 0:
            pl.semaphore_wait(barrier, len(XY) + len(ZK))
        for i in range(len(XY)):
            plane_copy(q, i).start()
        recv[q][cols(c, CHUNK), :] = send[q, cols(c, CHUNK), :]

    for i in (3, 4, 5, 6):
        loads[i].wait()
    req_owner = rown_v[...]
    req_slot = rslot_v[...]
    for o in range(REQS):
        wanted = jnp.sum(jnp.where(req_owner == o, req_slot.astype(F32), 0.0), axis=1, keepdims=True)
        slot_out[o] = jnp.broadcast_to(wanted, (8, 128)).astype(I32)
    for i in range(len(ZK)):
        slot_copy(i).start()
    slot_in[r] = slot_out[r]

    starts, counts = request_bounds(count_v[...].astype(F32))
    packed = iota((LIVE, CB), 0).astype(F32)
    lane = iota((LIVE, CB), 1).astype(F32)
    lane_owner = iota((LIVE, CB), 1) // CHUNK
    id_sum = jnp.zeros((LIVE, CB), F32)
    owner_sum = jnp.zeros((LIVE, CB), F32)
    req_owner_f = req_owner.astype(F32)
    for j in range(REQS):
        place = packed - starts[j]
        hit = jnp.logical_and(place == lane, lane < counts[j])
        id_sum = id_sum + jnp.where(hit, ids_v[0:1, j * CB : (j + 1) * CB].astype(F32), 0.0)
        inside = jnp.logical_and(place >= 0.0, place < counts[j])
        owner_sum = owner_sum + jnp.where(inside, req_owner_f[:, j : j + 1], 0.0)
    mask[...] = jnp.where(owner_sum == lane_owner.astype(F32), 1.0, 0.0)
    ids = jnp.sum(id_sum, axis=1, keepdims=True)
    for n in range(D // 128):
        word = (iota((LIVE, 128), 1) + n * 128).astype(F32)
        onehot[:, n * 128 : (n + 1) * 128] = jnp.where(ids == word, 1.0, 0.0).astype(BF16)

    loads[7].wait()

    def embed(n):
        emb[:, cols(n, 256)] = dot(onehot[...], table[:, cols(n, 256)]).astype(BF16)

    loop(D // 256, embed)
    emb_copy = pltpu.make_async_copy(emb, emb_h, emb_sem)
    emb_copy.start()

    def norm_emb(i):
        rows = cols(i, 64)
        cn[rows, :] = norm(emb[rows, :].astype(F32)).astype(BF16)

    loop(LIVE // 64, norm_emb)
    loads[8].wait()

    def project_q(n):
        query[:, cols(n, 256)] = silu(dot(cn[...], wqu[:, cols(n, 256)])).astype(BF16)
        gate[:, cols(n, 256)] = silu(dot(cn[...], wqu[:, pl.ds(pl.multiple_of(D + n * 256, 256), 256)])).astype(BF16)

    loop(D // 256, project_q)
    loads[9].wait()

    def project_kv(n):
        skv[:, cols(n, 256)] = silu(dot(cn[...], wkv[:, cols(n, 256)])).astype(BF16)

    loop(2 * D // 256, project_kv)

    def self_attend(h):
        head = cols(h, HEAD_DIM)
        product = query[:, head].astype(F32) * skv[:, head].astype(F32)
        weight = silu(jnp.sum(product, axis=1, keepdims=True) * SCALE)
        value = skv[:, pl.ds(pl.multiple_of(D + h * HEAD_DIM, HEAD_DIM), HEAD_DIM)].astype(F32)
        att[:, head] = weight * value

    loop(HEADS, self_attend)

    for i in range(len(ZK)):
        slot_copy(i).wait_recv()
    lane_row = iota((CHUNK, USERS * CHUNK), 1).astype(F32)
    step_s = iota((CHUNK, USERS * CHUNK), 0).astype(F32)
    for o in range(REQS):
        slot = slot_in[o][0:1, 0:1].astype(F32)
        hit = lane_row == slot * float(CHUNK) + step_s
        select[o * CHUNK : (o + 1) * CHUNK, :] = jnp.where(hit, 1.0, 0.0).astype(BF16)

    def attend_chunk(q):
        for i in range(len(ZK)):
            column_copy(q, i).wait_recv()

        def project(n):
            kvr[:, cols(n, 512)] = silu(dot(back[q][...], wkv[:, cols(n, 512)])).astype(BF16)

        loop(2 * D // 512, project)

        def attend(h):
            head = cols(h, HEAD_DIM)
            weight = silu(dot_nt(query[:, head], kvr[:, head]) * SCALE) * mask[...]
            value = kvr[:, pl.ds(pl.multiple_of(D + h * HEAD_DIM, HEAD_DIM), HEAD_DIM)]
            att[:, head] += dot(weight.astype(BF16), value)

        loop(HEADS, attend)

    for q in range(CHUNKS):
        for i in range(len(XY)):
            plane_copy(q, i).wait_recv()
        for n in range(2):
            stage[q, :, n * 512 : (n + 1) * 512] = dot(select[...], recv[q][:, n * 512 : (n + 1) * 512]).astype(BF16)
        for i in range(len(ZK)):
            column_copy(q, i).start()
        back[q][cols(r, CHUNK), :] = stage[q, cols(r, CHUNK), :]

        def project(n, q=q):
            block = silu(dot(recv[q][...], wkv[:, cols(n, 256)])).astype(BF16)
            kv[q, :, :, cols(n, 256)] = block.reshape(USERS, CHUNK, 256)

        loop(2 * D // 256, project)
        pltpu.make_async_copy(kv.at[q], cache_h.at[:, pl.ds(q * CHUNK, CHUNK), :], out_sem.at[q]).start()
        attend_chunk(q)

    def finish(i):
        rows = cols(i, 64)
        gated[rows, :] = (norm(att[rows, :]) * gate[rows, :].astype(F32)).astype(BF16)

    loop(LIVE // 64, finish)
    gated_copy = pltpu.make_async_copy(gated, gated_h, gated_sem)
    gated_copy.start()
    for i in range(len(ZK)):
        slot_copy(i).wait_send()
    for q in range(CHUNKS):
        for i in range(len(XY)):
            plane_copy(q, i).wait_send()
        for i in range(len(ZK)):
            column_copy(q, i).wait_send()
        pltpu.make_async_copy(kv.at[q], cache_h.at[:, pl.ds(q * CHUNK, CHUNK), :], out_sem.at[q]).wait()
    emb_copy.wait()
    gated_copy.wait()


def exchange(feats, lens, owners, ids, counts, req_owner, req_slot, table, w_qu, w_kv):
    any_spec = pl.BlockSpec(memory_space=pl.ANY)
    vmem = pltpu.VMEM
    return pl.pallas_call(
        exchange_kernel,
        out_shape=(
            jax.ShapeDtypeStruct((USERS, HIST, 2 * D), BF16),
            jax.ShapeDtypeStruct((LIVE, D), BF16),
            jax.ShapeDtypeStruct((LIVE, D), BF16),
        ),
        in_specs=[any_spec] * 10,
        out_specs=(any_spec,) * 3,
        scratch_shapes=[
            vmem((ROWS, D), BF16),
            vmem((1, USERS), I32), vmem((1, USERS), I32), vmem((1, REQS * CB), I32), vmem((1, REQS), I32),
            vmem((1, REQS), I32), vmem((1, REQS), I32),
            vmem((D, D), BF16), vmem((D, 2 * D), BF16), vmem((D, 2 * D), BF16),
            vmem((ROWS, D), BF16),
            vmem((CHUNKS, USERS * CHUNK, ROWS), BF16),
            vmem((CHUNKS, USERS * CHUNK, D), BF16),
        ]
        + [vmem((USERS * CHUNK, D), BF16)] * CHUNKS
        + [
            vmem((REQS, 8, 128), I32), vmem((REQS, 8, 128), I32),
            vmem((REQS * CHUNK, USERS * CHUNK), BF16),
            vmem((CHUNKS, REQS * CHUNK, D), BF16),
        ]
        + [vmem((REQS * CHUNK, D), BF16)] * CHUNKS
        + [
            vmem((CHUNKS, USERS, CHUNK, 2 * D), BF16),
            vmem((REQS * CHUNK, 2 * D), BF16),
            vmem((LIVE, D), BF16), vmem((LIVE, D), BF16), vmem((LIVE, D), BF16),
            vmem((LIVE, D), BF16), vmem((LIVE, D), BF16), vmem((LIVE, 2 * D), BF16),
            vmem((LIVE, D), F32), vmem((LIVE, CB), F32), vmem((LIVE, D), BF16),
            pltpu.SemaphoreType.DMA((10,)),
            pltpu.SemaphoreType.DMA((CHUNKS, len(XY))), pltpu.SemaphoreType.DMA((CHUNKS, len(XY))),
            pltpu.SemaphoreType.DMA((CHUNKS, len(ZK))), pltpu.SemaphoreType.DMA((CHUNKS, len(ZK))),
            pltpu.SemaphoreType.DMA((len(ZK),)), pltpu.SemaphoreType.DMA((len(ZK),)),
            pltpu.SemaphoreType.DMA((CHUNKS,)), pltpu.SemaphoreType.DMA, pltpu.SemaphoreType.DMA,
        ],
        compiler_params=pltpu.CompilerParams(collective_id=0, has_side_effects=True, vmem_limit_bytes=52 << 20),
        cost_estimate=pl.CostEstimate(flops=13 << 30, bytes_accessed=20 << 20, transcendentals=8 << 20),
        name="exchange",
    )(feats, lens, owners, ids, counts, req_owner, req_slot, table, w_qu, w_kv)


def output_kernel(cache_in, gated_h, emb_h, wout_h, count_h, cache_out, cand_h, gated, emb, wout, count_v, res, pick, out, sem, cache_sem, out_sem):
    pairs = [(count_h, count_v), (gated_h, gated), (wout_h, wout), (emb_h, emb)]
    loads = [pltpu.make_async_copy(src, dst, sem.at[i]) for i, (src, dst) in enumerate(pairs)]
    for copy in loads:
        copy.start()
    moves = [
        pltpu.make_async_copy(cache_in.at[pl.ds(i * 4, 4)], cache_out.at[pl.ds(i * 4, 4)], cache_sem.at[i]) for i in range(4)
    ]
    for copy in moves:
        copy.start()
    loads[0].wait()
    starts, counts = request_bounds(count_v[...].astype(F32))
    packed = iota((CB, LIVE), 1).astype(F32)
    slot = iota((CB, LIVE), 0).astype(F32)
    for j in range(REQS):
        hit = jnp.logical_and(packed - starts[j] == slot, slot < counts[j])
        pick[j * CB : (j + 1) * CB, :] = jnp.where(hit, 1.0, 0.0).astype(BF16)
    for i in (1, 2, 3):
        loads[i].wait()

    def project(n):
        res[:, cols(n, 256)] = (dot(gated[...], wout[:, cols(n, 256)]) + emb[:, cols(n, 256)].astype(F32)).astype(BF16)

    loop(D // 256, project)

    def out_copy(j):
        rows = pl.ds(j * 256, 256)
        return pltpu.make_async_copy(out.at[rows], cand_h.at[rows], out_sem.at[j])

    for j in range(4):
        rows = slice(j * 256, (j + 1) * 256)
        for n in range(2):
            out[rows, n * 512 : (n + 1) * 512] = dot(pick[rows, :], res[:, n * 512 : (n + 1) * 512]).astype(BF16)
        out_copy(j).start()
    for j in range(4):
        out_copy(j).wait()
    for copy in moves:
        copy.wait()


def output(cache, gated, emb, w_out, counts):
    any_spec = pl.BlockSpec(memory_space=pl.ANY)
    vmem = pltpu.VMEM
    return pl.pallas_call(
        output_kernel,
        out_shape=(
            jax.ShapeDtypeStruct((USERS, HIST, 2 * D), BF16),
            jax.ShapeDtypeStruct((REQS * CB, D), BF16),
        ),
        in_specs=[any_spec] * 5,
        out_specs=(any_spec,) * 2,
        scratch_shapes=[
            vmem((LIVE, D), BF16), vmem((LIVE, D), BF16), vmem((D, D), BF16), vmem((1, REQS), I32),
            vmem((LIVE, D), BF16), vmem((REQS * CB, LIVE), BF16), vmem((REQS * CB, D), BF16),
            pltpu.SemaphoreType.DMA((4,)), pltpu.SemaphoreType.DMA((4,)), pltpu.SemaphoreType.DMA((4,)),
        ],
        compiler_params=pltpu.CompilerParams(vmem_limit_bytes=24 << 20),
        cost_estimate=pl.CostEstimate(flops=2 << 30, bytes_accessed=16 << 20, transcendentals=0),
        name="output",
    )(cache, gated, emb, w_out, counts)


def body(event_feats, hist_len, user_owner, cand_ids, cand_count, req_owner, req_slot, table, w_qu, w_kv, w_out):
    cache, gated, emb = exchange(
        event_feats[0], hist_len, user_owner, cand_ids, cand_count, req_owner, req_slot, table, w_qu, w_kv
    )
    cache, cand_out = output(cache, gated, emb, w_out, cand_count)
    return (cache[None], cand_out[None])


def solution(mesh):
    in_specs = (
        P(("req", "cache"), None, None),
        P(("req", "cache"), None),
        P(("req", "cache"), None),
        P(("req", "cache"), None),
        P(("req", "cache"), None),
        P(("req", "cache"), None),
        P(("req", "cache"), None),
        P(),
        P(),
        P(),
        P(),
    )
    out_specs = (P(("req", "cache"), None, None, None), P(("req", "cache"), None, None))
    return jax.shard_map(body, mesh=mesh, in_specs=in_specs, out_specs=out_specs, check_vma=False)
```

```python
import jax
import jax.numpy as jnp
from jax import lax
from jax.experimental import pallas as pl
from jax.experimental.pallas import tpu as pltpu
from jax.sharding import PartitionSpec as P

D = 1024
HEADS = 8
HEAD_DIM = 128
HIST = 64
CB = 128
USERS = 16
REQS = 8
ROWS = 512
LIVE = 512
CHUNK = 16
CHUNKS = HIST // CHUNK
SCALE = HEAD_DIM ** (-0.5)
MESH = pl.DeviceIdType.MESH
F32 = jnp.float32
BF16 = jnp.bfloat16
I32 = jnp.int32

XY = [(2, 2), (0, 2), (2, 0), (3, 1), (1, 3), (3, 3), (1, 1), (2, 3), (3, 2), (2, 1), (1, 2), (3, 0), (0, 3), (1, 0), (0, 1)]
ZK = [(2, 0), (2, 1), (1, 0), (3, 0), (1, 1), (3, 1), (0, 1)]


def in_hbm(array):
    return pltpu.with_memory_space_constraint(array, pltpu.HBM)


def iota(shape, dim):
    return lax.broadcasted_iota(I32, shape, dim)


def silu(x):
    half = 0.5 * x
    return half + half * jnp.tanh(half)


def norm(x):
    mean = jnp.sum(x, axis=-1, keepdims=True) * (1.0 / D)
    centred = x - mean
    spread = jnp.sum(centred * centred, axis=-1, keepdims=True) * (1.0 / D)
    return centred * lax.rsqrt(spread + 1e-06)


def dot(a, b):
    return jnp.dot(a, b, preferred_element_type=F32)


def dot_nt(a, b):
    return lax.dot_general(a, b, (((1,), (1,)), ((), ())), preferred_element_type=F32)


def cols(i, width):
    return pl.ds(pl.multiple_of(i * width, width), width)


def request_bounds(counts):
    lane = iota((1, REQS), 1)
    starts = [jnp.sum(jnp.where(lane < j, counts, 0.0), axis=1, keepdims=True) for j in range(REQS)]
    lengths = [jnp.sum(jnp.where(lane == j, counts, 0.0), axis=1, keepdims=True) for j in range(REQS)]
    return starts, lengths


def exchange_kernel(
    feats_h, len_h, own_h, ids_h, count_h, rown_h, rslot_h, table_h, wqu_h, wkv_h,
    kv, gated, emb,
    feats, len_v, own_v, ids_v, count_v, rown_v, rslot_v, table, wqu, wkv,
    hn, pick, send, recv0, recv1, recv2, recv3, slot_out, slot_in, select,
    stage, back0, back1, back2, back3, kvr,
    onehot, cn, query, gate, skv, att, mask,
    load_sem, ss1, rs1, ss2, rs2, sss, rss,
):
    r = lax.axis_index("req")
    c = lax.axis_index("cache")
    z, k = r // 2, lax.rem(r, 2)
    y, x = c // 4, lax.rem(c, 4)
    recv = [recv0, recv1, recv2, recv3]
    back = [back0, back1, back2, back3]

    def plane(offset):
        dy, dx = offset
        return lax.rem(y + dy, 4) * 4 + lax.rem(x + dx, 4)

    def column(offset):
        dz, dk = offset
        return lax.rem(z + dz, 4) * 2 + lax.rem(k + dk, 2)

    barrier = pltpu.get_barrier_semaphore()
    for offset in XY:
        pl.semaphore_signal(barrier, inc=1, device_id=(r, plane(offset)), device_id_type=MESH)
    for offset in ZK:
        pl.semaphore_signal(barrier, inc=1, device_id=(column(offset), c), device_id_type=MESH)

    pairs = [
        (len_h, len_v), (own_h, own_v), (feats_h, feats), (count_h, count_v), (ids_h, ids_v), (rown_h, rown_v), (rslot_h, rslot_v),
        (table_h, table), (wqu_h, wqu), (wkv_h, wkv),
    ]
    loads = [pltpu.make_async_copy(src, dst, load_sem.at[i]) for i, (src, dst) in enumerate(pairs)]
    for copy in loads:
        copy.start()

    loads[0].wait()
    loads[1].wait()
    lengths = len_v[...].astype(F32)
    owner = own_v[...]
    lane_j = iota((USERS, USERS), 1)
    mine = owner == iota((USERS, USERS), 0)
    order = jnp.sum(jnp.where(mine, lane_j.astype(F32), 0.0), axis=1, keepdims=True)
    length_of = jnp.sum(jnp.where(mine, lengths, 0.0), axis=1, keepdims=True)
    start_of = jnp.sum(jnp.where(lane_j.astype(F32) < order, lengths, 0.0), axis=1, keepdims=True)
    row = iota((CHUNK, ROWS), 1).astype(F32)
    step_t = iota((CHUNK, ROWS), 0).astype(F32)
    for o in range(USERS):
        place = row - start_of[o : o + 1, :]
        live = place < length_of[o : o + 1, :]
        for q in range(CHUNKS):
            hit = jnp.logical_and(place == step_t + float(q * CHUNK), live)
            pick[q, o * CHUNK : (o + 1) * CHUNK, :] = jnp.where(hit, 1.0, 0.0).astype(BF16)

    loads[2].wait()

    for i in range(ROWS // 64):
        rows = slice(i * 64, (i + 1) * 64)
        hn[rows, :] = norm(feats[rows, :].astype(F32)).astype(BF16)

    def slot_copy(i):
        to = column(ZK[i])
        return pltpu.make_async_remote_copy(
            src_ref=slot_out.at[to], dst_ref=slot_in.at[r], send_sem=sss.at[i], recv_sem=rss.at[i],
            device_id=(to, c), device_id_type=MESH,
        )

    def plane_copy(q, i):
        to = plane(XY[i])
        return pltpu.make_async_remote_copy(
            src_ref=send.at[q, cols(to, CHUNK), :], dst_ref=recv[q].at[cols(c, CHUNK), :],
            send_sem=ss1.at[q, i], recv_sem=rs1.at[q, i], device_id=(r, to), device_id_type=MESH,
        )

    def column_copy(q, i):
        to = column(ZK[i])
        return pltpu.make_async_remote_copy(
            src_ref=stage.at[q, cols(to, CHUNK), :], dst_ref=back[q].at[cols(r, CHUNK), :],
            send_sem=ss2.at[q, i], recv_sem=rs2.at[q, i], device_id=(to, c), device_id_type=MESH,
        )

    for q in range(CHUNKS):
        send[q] = dot(pick[q], hn[...]).astype(BF16)
        if q == 0:
            pl.semaphore_wait(barrier, len(XY) + len(ZK))
        for i in range(len(XY)):
            plane_copy(q, i).start()
        recv[q][cols(c, CHUNK), :] = send[q, cols(c, CHUNK), :]

    for i in (3, 4, 5, 6):
        loads[i].wait()
    req_owner = rown_v[...]
    req_slot = rslot_v[...]
    for o in range(REQS):
        wanted = jnp.sum(jnp.where(req_owner == o, req_slot.astype(F32), 0.0), axis=1, keepdims=True)
        slot_out[o] = jnp.broadcast_to(wanted, (8, 128)).astype(I32)
    for i in range(len(ZK)):
        slot_copy(i).start()
    slot_in[r] = slot_out[r]

    starts, counts = request_bounds(count_v[...].astype(F32))
    packed = iota((LIVE, CB), 0).astype(F32)
    lane = iota((LIVE, CB), 1).astype(F32)
    lane_owner = iota((LIVE, CB), 1) // CHUNK
    id_sum = jnp.zeros((LIVE, CB), F32)
    owner_sum = jnp.zeros((LIVE, CB), F32)
    req_owner_f = req_owner.astype(F32)
    for j in range(REQS):
        place = packed - starts[j]
        hit = jnp.logical_and(place == lane, lane < counts[j])
        id_sum = id_sum + jnp.where(hit, ids_v[0:1, j * CB : (j + 1) * CB].astype(F32), 0.0)
        inside = jnp.logical_and(place >= 0.0, place < counts[j])
        owner_sum = owner_sum + jnp.where(inside, req_owner_f[:, j : j + 1], 0.0)
    mask[...] = jnp.where(owner_sum == lane_owner.astype(F32), 1.0, 0.0)
    ids = jnp.sum(id_sum, axis=1, keepdims=True)
    for n in range(D // 128):
        word = (iota((LIVE, 128), 1) + n * 128).astype(F32)
        onehot[:, n * 128 : (n + 1) * 128] = jnp.where(ids == word, 1.0, 0.0).astype(BF16)

    loads[7].wait()

    emb[...] = dot(onehot[...], table[...]).astype(BF16)
    for i in range(LIVE // 64):
        rows = slice(i * 64, (i + 1) * 64)
        cn[rows, :] = norm(emb[rows, :].astype(F32)).astype(BF16)
    loads[8].wait()
    query[...] = silu(dot(cn[...], wqu[:, :D])).astype(BF16)
    gate[...] = silu(dot(cn[...], wqu[:, D:])).astype(BF16)
    loads[9].wait()
    skv[...] = silu(dot(cn[...], wkv[...])).astype(BF16)
    for h in range(HEADS):
        head = slice(h * HEAD_DIM, (h + 1) * HEAD_DIM)
        value = slice(D + h * HEAD_DIM, D + (h + 1) * HEAD_DIM)
        product = query[:, head].astype(F32) * skv[:, head].astype(F32)
        weight = silu(jnp.sum(product, axis=1, keepdims=True) * SCALE)
        att[:, head] = weight * skv[:, value].astype(F32)

    for i in range(len(ZK)):
        slot_copy(i).wait_recv()
    lane_row = iota((CHUNK, USERS * CHUNK), 1).astype(F32)
    step_s = iota((CHUNK, USERS * CHUNK), 0).astype(F32)
    for o in range(REQS):
        slot = slot_in[o][0:1, 0:1].astype(F32)
        hit = lane_row == slot * float(CHUNK) + step_s
        select[o * CHUNK : (o + 1) * CHUNK, :] = jnp.where(hit, 1.0, 0.0).astype(BF16)

    def attend_chunk(q):
        for i in range(len(ZK)):
            column_copy(q, i).wait_recv()
        kvr[...] = silu(dot(back[q][...], wkv[...])).astype(BF16)
        for h in range(HEADS):
            head = slice(h * HEAD_DIM, (h + 1) * HEAD_DIM)
            value = slice(D + h * HEAD_DIM, D + (h + 1) * HEAD_DIM)
            weight = silu(dot_nt(query[:, head], kvr[:, head]) * SCALE) * mask[...]
            att[:, head] += dot(weight.astype(BF16), kvr[:, value])

    for q in range(CHUNKS):
        for i in range(len(XY)):
            plane_copy(q, i).wait_recv()
        stage[q] = dot(select[...], recv[q][...]).astype(BF16)
        for i in range(len(ZK)):
            column_copy(q, i).start()
        back[q][cols(r, CHUNK), :] = stage[q, cols(r, CHUNK), :]
        block = silu(dot(recv[q][...], wkv[...])).astype(BF16)
        kv[:, q * CHUNK : (q + 1) * CHUNK, :] = block.reshape(USERS, CHUNK, 2 * D)
        if q > 0:
            attend_chunk(q - 1)
    attend_chunk(CHUNKS - 1)

    for i in range(LIVE // 64):
        rows = slice(i * 64, (i + 1) * 64)
        gated[rows, :] = (norm(att[rows, :]) * gate[rows, :].astype(F32)).astype(BF16)
    for i in range(len(ZK)):
        slot_copy(i).wait_send()
    for q in range(CHUNKS):
        for i in range(len(XY)):
            plane_copy(q, i).wait_send()
        for i in range(len(ZK)):
            column_copy(q, i).wait_send()


def exchange(feats, lens, owners, ids, counts, req_owner, req_slot, table, w_qu, w_kv):
    any_spec = pl.BlockSpec(memory_space=pl.ANY)
    vmem = pltpu.VMEM
    return pl.pallas_call(
        exchange_kernel,
        out_shape=(
            pltpu.VMEM((USERS, HIST, 2 * D), BF16),
            pltpu.VMEM((LIVE, D), BF16),
            pltpu.VMEM((LIVE, D), BF16),
        ),
        in_specs=[any_spec] * 10,
        out_specs=(pl.BlockSpec(memory_space=pltpu.VMEM),) * 3,
        scratch_shapes=[
            vmem((ROWS, D), BF16),
            vmem((1, USERS), I32), vmem((1, USERS), I32), vmem((1, REQS * CB), I32), vmem((1, REQS), I32),
            vmem((1, REQS), I32), vmem((1, REQS), I32),
            vmem((D, D), BF16), vmem((D, 2 * D), BF16), vmem((D, 2 * D), BF16),
            vmem((ROWS, D), BF16),
            vmem((CHUNKS, USERS * CHUNK, ROWS), BF16),
            vmem((CHUNKS, USERS * CHUNK, D), BF16),
        ]
        + [vmem((USERS * CHUNK, D), BF16)] * CHUNKS
        + [
            vmem((REQS, 8, 128), I32), vmem((REQS, 8, 128), I32),
            vmem((REQS * CHUNK, USERS * CHUNK), BF16),
            vmem((CHUNKS, REQS * CHUNK, D), BF16),
        ]
        + [vmem((REQS * CHUNK, D), BF16)] * CHUNKS
        + [
            vmem((REQS * CHUNK, 2 * D), BF16),
            vmem((LIVE, D), BF16), vmem((LIVE, D), BF16),
            vmem((LIVE, D), BF16), vmem((LIVE, D), BF16), vmem((LIVE, 2 * D), BF16),
            vmem((LIVE, D), F32), vmem((LIVE, CB), F32),
            pltpu.SemaphoreType.DMA((10,)),
            pltpu.SemaphoreType.DMA((CHUNKS, len(XY))), pltpu.SemaphoreType.DMA((CHUNKS, len(XY))),
            pltpu.SemaphoreType.DMA((CHUNKS, len(ZK))), pltpu.SemaphoreType.DMA((CHUNKS, len(ZK))),
            pltpu.SemaphoreType.DMA((len(ZK),)), pltpu.SemaphoreType.DMA((len(ZK),)),
        ],
        compiler_params=pltpu.CompilerParams(collective_id=0, has_side_effects=True, vmem_limit_bytes=46 << 20),
        cost_estimate=pl.CostEstimate(flops=13 << 30, bytes_accessed=20 << 20, transcendentals=8 << 20),
        name="exchange",
    )(feats, lens, owners, ids, counts, req_owner, req_slot, table, w_qu, w_kv)


def output_kernel(cache_in, gated, emb, wout, count_h, cache_out, cand_h, count_v, res, pick, out, sem, cache_sem, out_sem):
    load = pltpu.make_async_copy(count_h, count_v, sem)
    load.start()
    moves = [
        pltpu.make_async_copy(cache_in.at[pl.ds(i * 4, 4)], cache_out.at[pl.ds(i * 4, 4)], cache_sem.at[i]) for i in range(4)
    ]
    for copy in moves:
        copy.start()
    res[...] = (dot(gated[...], wout[...]) + emb[...].astype(F32)).astype(BF16)
    load.wait()
    starts, counts = request_bounds(count_v[...].astype(F32))
    packed = iota((CB, LIVE), 1).astype(F32)
    slot = iota((CB, LIVE), 0).astype(F32)
    for j in range(REQS):
        hit = jnp.logical_and(packed - starts[j] == slot, slot < counts[j])
        pick[j * CB : (j + 1) * CB, :] = jnp.where(hit, 1.0, 0.0).astype(BF16)

    def out_copy(j):
        rows = pl.ds(j * 256, 256)
        return pltpu.make_async_copy(out.at[rows], cand_h.at[rows], out_sem.at[j])

    for j in range(4):
        rows = slice(j * 256, (j + 1) * 256)
        out[rows, :] = dot(pick[rows, :], res[...]).astype(BF16)
        out_copy(j).start()
    for j in range(4):
        out_copy(j).wait()
    for copy in moves:
        copy.wait()


def output(cache, gated, emb, w_out, counts):
    any_spec = pl.BlockSpec(memory_space=pl.ANY)
    vmem = pltpu.VMEM
    return pl.pallas_call(
        output_kernel,
        out_shape=(
            jax.ShapeDtypeStruct((USERS, HIST, 2 * D), BF16),
            jax.ShapeDtypeStruct((REQS * CB, D), BF16),
        ),
        in_specs=[pl.BlockSpec(memory_space=vmem)] * 4 + [any_spec],
        out_specs=(any_spec,) * 2,
        scratch_shapes=[
            vmem((1, REQS), I32),
            vmem((LIVE, D), BF16), vmem((REQS * CB, LIVE), BF16), vmem((REQS * CB, D), BF16),
            pltpu.SemaphoreType.DMA, pltpu.SemaphoreType.DMA((4,)), pltpu.SemaphoreType.DMA((4,)),
        ],
        compiler_params=pltpu.CompilerParams(vmem_limit_bytes=24 << 20),
        cost_estimate=pl.CostEstimate(flops=2 << 30, bytes_accessed=16 << 20, transcendentals=0),
        name="output",
    )(cache, gated, emb, w_out, in_hbm(counts))


def body(event_feats, hist_len, user_owner, cand_ids, cand_count, req_owner, req_slot, table, w_qu, w_kv, w_out):
    cache, gated, emb = exchange(
        *(in_hbm(a) for a in (event_feats[0], hist_len, user_owner, cand_ids, cand_count, req_owner, req_slot, table, w_qu, w_kv))
    )
    cache, cand_out = output(cache, gated, emb, w_out, cand_count)
    return (cache[None], cand_out[None])


def solution(mesh):
    in_specs = (
        P(("req", "cache"), None, None),
        P(("req", "cache"), None),
        P(("req", "cache"), None),
        P(("req", "cache"), None),
        P(("req", "cache"), None),
        P(("req", "cache"), None),
        P(("req", "cache"), None),
        P(),
        P(),
        P(),
        P(),
    )
    out_specs = (P(("req", "cache"), None, None, None), P(("req", "cache"), None, None))
    return jax.shard_map(body, mesh=mesh, in_specs=in_specs, out_specs=out_specs, check_vma=False)
```

```python
import jax
import jax.numpy as jnp
from jax import lax
from jax.experimental import pallas as pl
from jax.experimental.pallas import tpu as pltpu
from jax.sharding import PartitionSpec as P

D = 1024
HEADS = 8
HEAD_DIM = 128
HIST = 64
CB = 128
USERS = 16
REQS = 8
ROWS = 512
LIVE = 512
CHUNK = (16, 16, 16, 16)
CHUNKS = len(CHUNK)
FIRST = tuple(sum(CHUNK[:q]) for q in range(CHUNKS))
LAST = CHUNKS - 1
WINDOW = 256
SCALE = HEAD_DIM ** (-0.5)
MESH = pl.DeviceIdType.MESH
F32 = jnp.float32
BF16 = jnp.bfloat16
I32 = jnp.int32

XY = [(2, 2), (0, 2), (2, 0), (3, 1), (1, 3), (3, 3), (1, 1), (2, 3), (3, 2), (2, 1), (1, 2), (3, 0), (0, 3), (1, 0), (0, 1)]
ZK = [(2, 0), (2, 1), (1, 0), (3, 0), (1, 1), (3, 1), (0, 1)]


def in_hbm(array):
    return pltpu.with_memory_space_constraint(array, pltpu.HBM)


def iota(shape, dim):
    return lax.broadcasted_iota(I32, shape, dim)


def silu(x):
    half = 0.5 * x
    return half + half * jnp.tanh(half)


def masked_silu(x, half_scale):
    half = x * half_scale
    return (half + half * jnp.tanh(half)).astype(BF16)


def norm(x):
    mean = jnp.sum(x, axis=-1, keepdims=True) * (1.0 / D)
    centred = x - mean
    spread = jnp.sum(centred * centred, axis=-1, keepdims=True) * (1.0 / D)
    return centred * lax.rsqrt(spread + 1e-06)


def dot(a, b):
    return jnp.dot(a, b, preferred_element_type=F32)


def dot_nt(a, b):
    return lax.dot_general(a, b, (((1,), (1,)), ((), ())), preferred_element_type=F32)


def cols(i, width):
    return pl.ds(pl.multiple_of(i * width, width), width)


def request_bounds(counts):
    lane = iota((1, REQS), 1)
    starts = [jnp.sum(jnp.where(lane < j, counts, 0.0), axis=1, keepdims=True) for j in range(REQS)]
    lengths = [jnp.sum(jnp.where(lane == j, counts, 0.0), axis=1, keepdims=True) for j in range(REQS)]
    return starts, lengths


def exchange_kernel(
    feats_h, len_h, own_h, ids_h, count_h, rown_h, rslot_h, table_h, wqu_h, wkv_h, wout_h,
    kv, emb, query, gate, att, asked, wkv, wout, mask, spread,
    feats, len_v, own_v, ids_v, count_v, rown_v, rslot_v, table, wqu,
    hn, pick0, pick1, pick2, pick3, send0, send1, send2, send3, recv0, recv1, recv2, recv3, slot_out, slot_in, select,
    stage0, stage1, stage2, stage3, back0, back1, back2, back3, kvr, onehot, cn, skv,
    load_sem, ss1, rs1, ss2, rs2, sss, rss,
):
    r = lax.axis_index("req")
    c = lax.axis_index("cache")
    z, k = r // 2, lax.rem(r, 2)
    y, x = c // 4, lax.rem(c, 4)
    pick = [pick0, pick1, pick2, pick3]
    send = [send0, send1, send2, send3]
    recv = [recv0, recv1, recv2, recv3]
    stage = [stage0, stage1, stage2, stage3]
    back = [back0, back1, back2, back3]

    def plane(offset):
        dy, dx = offset
        return lax.rem(y + dy, 4) * 4 + lax.rem(x + dx, 4)

    def column(offset):
        dz, dk = offset
        return lax.rem(z + dz, 4) * 2 + lax.rem(k + dk, 2)

    pairs = [
        (feats_h, feats), (len_h, len_v), (own_h, own_v), (count_h, count_v), (ids_h, ids_v), (rown_h, rown_v), (rslot_h, rslot_v),
        (table_h, table), (wqu_h, wqu), (wkv_h, wkv), (wout_h, wout),
    ]
    loads = [pltpu.make_async_copy(src, dst, load_sem.at[i]) for i, (src, dst) in enumerate(pairs)]
    for i in (1, 2, 0):
        loads[i].start()

    barrier = pltpu.get_barrier_semaphore()
    for offset in XY:
        pl.semaphore_signal(barrier, inc=1, device_id=(r, plane(offset)), device_id_type=MESH)
    for offset in ZK:
        pl.semaphore_signal(barrier, inc=1, device_id=(column(offset), c), device_id_type=MESH)

    loads[1].wait()
    loads[2].wait()
    lengths = len_v[...].astype(F32)
    owner = own_v[...]
    lane_j = iota((USERS, USERS), 1)
    mine = owner == iota((USERS, USERS), 0)
    order = jnp.sum(jnp.where(mine, lane_j.astype(F32), 0.0), axis=1, keepdims=True)
    length_of = jnp.sum(jnp.where(mine, lengths, 0.0), axis=1, keepdims=True)
    start_of = jnp.sum(jnp.where(lane_j.astype(F32) < order, lengths, 0.0), axis=1, keepdims=True)

    def build_pick(q):
        n = CHUNK[q]
        row = iota((n, ROWS), 1).astype(F32)
        step = iota((n, ROWS), 0).astype(F32) + float(FIRST[q])
        for o in range(USERS):
            place = row - start_of[o : o + 1, :]
            hit = jnp.logical_and(place == step, place < length_of[o : o + 1, :])
            pick[q][o * n : (o + 1) * n, :] = jnp.where(hit, 1.0, 0.0).astype(BF16)

    def slot_copy(i):
        to = column(ZK[i])
        return pltpu.make_async_remote_copy(
            src_ref=slot_out.at[to], dst_ref=slot_in.at[r], send_sem=sss.at[i], recv_sem=rss.at[i],
            device_id=(to, c), device_id_type=MESH,
        )

    def plane_copy(q, i):
        to = plane(XY[i])
        return pltpu.make_async_remote_copy(
            src_ref=send[q].at[cols(to, CHUNK[q]), :], dst_ref=recv[q].at[cols(c, CHUNK[q]), :],
            send_sem=ss1.at[q, i], recv_sem=rs1.at[q, i], device_id=(r, to), device_id_type=MESH,
        )

    def column_copy(q, i):
        to = column(ZK[i])
        return pltpu.make_async_remote_copy(
            src_ref=stage[q].at[cols(to, CHUNK[q]), :], dst_ref=back[q].at[cols(r, CHUNK[q]), :],
            send_sem=ss2.at[q, i], recv_sem=rs2.at[q, i], device_id=(to, c), device_id_type=MESH,
        )

    loads[0].wait()
    for i in range(ROWS // 64):
        rows = slice(i * 64, (i + 1) * 64)
        hn[rows, :] = norm(feats[rows, :].astype(F32)).astype(BF16)
    for q in range(CHUNKS):
        build_pick(q)
        send[q][...] = dot(pick[q][...], hn[...]).astype(BF16)
        if q == 0:
            pl.semaphore_wait(barrier, len(XY) + len(ZK))
        for i in range(len(XY)):
            plane_copy(q, i).start()
        if q == 0:
            for i in range(3, len(loads)):
                loads[i].start()
        own_rows = cols(c, CHUNK[q])
        recv[q][own_rows, :] = send[q][own_rows, :]

    for i in (3, 4, 5, 6):
        loads[i].wait()
    req_owner = rown_v[...]
    req_slot = rslot_v[...]
    for o in range(REQS):
        wanted = jnp.sum(jnp.where(req_owner == o, req_slot.astype(F32), 0.0), axis=1, keepdims=True)
        slot_out[o] = jnp.broadcast_to(wanted, (8, 128)).astype(I32)
    for i in range(len(ZK)):
        slot_copy(i).start()
    slot_in[r] = slot_out[r]

    starts, counts = request_bounds(count_v[...].astype(F32))
    packed = iota((LIVE, CB), 0).astype(F32)
    lane = iota((LIVE, CB), 1).astype(F32)
    id_sum = jnp.zeros((LIVE, CB), F32)
    owner_sum = jnp.zeros((LIVE, CB), F32)
    req_owner_f = req_owner.astype(F32)
    for j in range(REQS):
        place = packed - starts[j]
        hit = jnp.logical_and(place == lane, lane < counts[j])
        id_sum = id_sum + jnp.where(hit, ids_v[0:1, j * CB : (j + 1) * CB].astype(F32), 0.0)
        inside = jnp.logical_and(place >= 0.0, place < counts[j])
        owner_sum = owner_sum + jnp.where(inside, req_owner_f[:, j : j + 1], 0.0)
    mask[...] = jnp.where(owner_sum == (iota((LIVE, CB), 1) // CHUNK[1]).astype(F32), 0.5 * SCALE, 0.0)
    ids = jnp.sum(id_sum, axis=1, keepdims=True)
    for n in range(D // 128):
        word = (iota((LIVE, 128), 1) + n * 128).astype(F32)
        onehot[:, n * 128 : (n + 1) * 128] = jnp.where(ids == word, 1.0, 0.0).astype(BF16)

    loads[7].wait()
    emb[...] = dot(onehot[...], table[...]).astype(BF16)
    for i in range(LIVE // 64):
        rows = slice(i * 64, (i + 1) * 64)
        cn[rows, :] = norm(emb[rows, :].astype(F32)).astype(BF16)
    loads[8].wait()
    query[...] = silu(dot(cn[...], wqu[:, :D])).astype(BF16)
    gate[...] = silu(dot(cn[...], wqu[:, D:])).astype(BF16)
    loads[9].wait()
    skv[...] = silu(dot(cn[...], wkv[...])).astype(BF16)
    for h in range(HEADS):
        head = slice(h * HEAD_DIM, (h + 1) * HEAD_DIM)
        value = slice(D + h * HEAD_DIM, D + (h + 1) * HEAD_DIM)
        product = query[:, head].astype(F32) * skv[:, head].astype(F32)
        weight = silu(jnp.sum(product, axis=1, keepdims=True) * SCALE)
        att[:, head] = weight * skv[:, value].astype(F32)

    slot = iota((CB, WINDOW), 0).astype(F32)
    shifted = iota((CB, WINDOW), 1).astype(F32) - slot
    for j in range(REQS):
        base = jnp.minimum(jnp.floor(starts[j] * (1.0 / 16.0)) * 16.0, float(LIVE - WINDOW))
        hit = jnp.logical_and(shifted == starts[j] - base, slot < counts[j])
        spread[j * CB : (j + 1) * CB, :] = jnp.where(hit, 1.0, 0.0).astype(BF16)

    for i in range(len(ZK)):
        slot_copy(i).wait_recv()
    n = CHUNK[0]
    lane_row = iota((n, USERS * n), 1).astype(F32)
    step = iota((n, USERS * n), 0).astype(F32)
    for o in range(REQS):
        slot = slot_in[o][0:1, 0:1].astype(F32)
        hit = lane_row == slot * float(n) + step
        select[o * n : (o + 1) * n, :] = jnp.where(hit, 1.0, 0.0).astype(BF16)

    def attend_chunk(q):
        for i in range(len(ZK)):
            column_copy(q, i).wait_recv()
        keys = slice(0, REQS * CHUNK[q])
        kvr[keys, :] = silu(dot(back[q][...], wkv[...])).astype(BF16)
        for h in range(HEADS):
            head = slice(h * HEAD_DIM, (h + 1) * HEAD_DIM)
            value = slice(D + h * HEAD_DIM, D + (h + 1) * HEAD_DIM)
            weight = masked_silu(dot_nt(query[:, head], kvr[keys, head]), mask[...])
            att[:, head] += dot(weight, kvr[keys, value])

    for q in range(CHUNKS):
        n = CHUNK[q]
        for i in range(len(XY)):
            plane_copy(q, i).wait_recv()
        stage[q][...] = dot(select[...], recv[q][...]).astype(BF16)
        for i in range(len(ZK)):
            column_copy(q, i).start()
        own_rows = cols(r, n)
        back[q][own_rows, :] = stage[q][own_rows, :]
        block = silu(dot(recv[q][...], wkv[...])).astype(BF16)
        kv[:, FIRST[q] : FIRST[q] + n, :] = block.reshape(USERS, n, 2 * D)
        if q > 0:
            attend_chunk(q - 1)

    for i in range(len(ZK)):
        slot_copy(i).wait_send()
    for q in range(CHUNKS):
        for i in range(len(XY)):
            plane_copy(q, i).wait_send()
        for i in range(len(ZK)):
            column_copy(q, i).wait_send()
    loads[10].wait()
    for i in range(len(ZK)):
        column_copy(LAST, i).wait_recv()
    asked[...] = back[LAST][...]


def exchange(feats, lens, owners, ids, counts, req_owner, req_slot, table, w_qu, w_kv, w_out):
    any_spec = pl.BlockSpec(memory_space=pl.ANY)
    vmem = pltpu.VMEM
    sems = pltpu.SemaphoreType.DMA
    outs = (
        vmem((USERS, HIST, 2 * D), BF16), vmem((LIVE, D), BF16), vmem((LIVE, D), BF16), vmem((LIVE, D), BF16),
        vmem((LIVE, D), F32), vmem((REQS * CHUNK[LAST], D), BF16), vmem((D, 2 * D), BF16), vmem((D, D), BF16),
        vmem((LIVE, REQS * CHUNK[LAST]), F32), vmem((REQS * CB, WINDOW), BF16),
    )
    return pl.pallas_call(
        exchange_kernel,
        out_shape=outs,
        in_specs=[any_spec] * 11,
        out_specs=(pl.BlockSpec(memory_space=vmem),) * len(outs),
        scratch_shapes=[
            vmem((ROWS, D), BF16),
            vmem((1, USERS), I32), vmem((1, USERS), I32), vmem((1, REQS * CB), I32), vmem((1, REQS), I32),
            vmem((1, REQS), I32), vmem((1, REQS), I32),
            vmem((D, D), BF16), vmem((D, 2 * D), BF16),
            vmem((ROWS, D), BF16),
        ]
        + [vmem((USERS * n, ROWS), BF16) for n in CHUNK]
        + [vmem((USERS * n, D), BF16) for n in CHUNK]
        + [vmem((USERS * n, D), BF16) for n in CHUNK]
        + [vmem((REQS, 8, 128), I32), vmem((REQS, 8, 128), I32)]
        + [vmem((REQS * n, USERS * n), BF16) for n in CHUNK[:1]]
        + [vmem((REQS * n, D), BF16) for n in CHUNK]
        + [vmem((REQS * n, D), BF16) for n in CHUNK]
        + [
            vmem((REQS * max(CHUNK), 2 * D), BF16),
            vmem((LIVE, D), BF16), vmem((LIVE, D), BF16), vmem((LIVE, 2 * D), BF16),
            sems((11,)),
            sems((CHUNKS, len(XY))), sems((CHUNKS, len(XY))),
            sems((CHUNKS, len(ZK))), sems((CHUNKS, len(ZK))),
            sems((len(ZK),)), sems((len(ZK),)),
        ],
        compiler_params=pltpu.CompilerParams(collective_id=0, has_side_effects=True, vmem_limit_bytes=40 << 20),
        cost_estimate=pl.CostEstimate(flops=13 << 30, bytes_accessed=20 << 20, transcendentals=8 << 20),
        name="exchange",
    )(feats, lens, owners, ids, counts, req_owner, req_slot, table, w_qu, w_kv, w_out)


def output_kernel(
    cache_in, emb, query, gate, att, asked, wkv, wout, mask, spread, count_h,
    cache_out, cand_h,
    count_s, mixed, gated, res, out,
    sem, cache_sem, out_sem,
):
    load = pltpu.make_async_copy(count_h, count_s, sem)
    load.start()
    moves = [
        pltpu.make_async_copy(cache_in.at[pl.ds(i * 4, 4)], cache_out.at[pl.ds(i * 4, 4)], cache_sem.at[i]) for i in range(4)
    ]
    for copy in moves:
        copy.start()

    block = silu(dot(asked[...], wkv[...])).astype(BF16)
    for h in range(HEADS):
        head = slice(h * HEAD_DIM, (h + 1) * HEAD_DIM)
        value = slice(D + h * HEAD_DIM, D + (h + 1) * HEAD_DIM)
        weight = masked_silu(dot_nt(query[:, head], block[:, head]), mask[...])
        mixed[:, head] = att[:, head] + dot(weight, block[:, value])
    for i in range(LIVE // 64):
        rows = slice(i * 64, (i + 1) * 64)
        gated[rows, :] = (norm(mixed[rows, :]) * gate[rows, :].astype(F32)).astype(BF16)
    res[...] = (dot(gated[...], wout[...]) + emb[...].astype(F32)).astype(BF16)

    def out_copy(j):
        rows = pl.ds(j * CB, CB)
        return pltpu.make_async_copy(out.at[rows], cand_h.at[rows], out_sem.at[j])

    load.wait()
    start = jnp.int32(0)
    for j in range(REQS):
        base = jnp.minimum((start // 16) * 16, LIVE - WINDOW)
        window = pl.ds(pl.multiple_of(base, 16), WINDOW)
        out[j * CB : (j + 1) * CB, :] = dot(spread[j * CB : (j + 1) * CB, :], res[window, :]).astype(BF16)
        out_copy(j).start()
        start = start + count_s[0, j]
    for j in range(REQS):
        out_copy(j).wait()
    for copy in moves:
        copy.wait()


def output(cache, emb, query, gate, att, asked, w_kv, w_out, mask, spread, counts):
    any_spec = pl.BlockSpec(memory_space=pl.ANY)
    vmem = pltpu.VMEM
    return pl.pallas_call(
        output_kernel,
        out_shape=(
            jax.ShapeDtypeStruct((USERS, HIST, 2 * D), BF16),
            jax.ShapeDtypeStruct((REQS * CB, D), BF16),
        ),
        in_specs=[pl.BlockSpec(memory_space=vmem)] * 10 + [any_spec],
        out_specs=(any_spec,) * 2,
        scratch_shapes=[
            pltpu.SMEM((1, REQS), I32),
            vmem((LIVE, D), F32), vmem((LIVE, D), BF16), vmem((LIVE, D), BF16), vmem((REQS * CB, D), BF16),
            pltpu.SemaphoreType.DMA, pltpu.SemaphoreType.DMA((4,)), pltpu.SemaphoreType.DMA((REQS,)),
        ],
        compiler_params=pltpu.CompilerParams(vmem_limit_bytes=24 << 20),
        cost_estimate=pl.CostEstimate(flops=3 << 30, bytes_accessed=16 << 20, transcendentals=0),
        name="output",
    )(cache, emb, query, gate, att, asked, w_kv, w_out, mask, spread, in_hbm(counts))


def body(event_feats, hist_len, user_owner, cand_ids, cand_count, req_owner, req_slot, table, w_qu, w_kv, w_out):
    held = exchange(
        *(in_hbm(a) for a in (event_feats[0], hist_len, user_owner, cand_ids, cand_count, req_owner, req_slot, table, w_qu, w_kv, w_out))
    )
    cache, cand_out = output(*held, cand_count)
    return (cache[None], cand_out[None])


def solution(mesh):
    in_specs = (
        P(("req", "cache"), None, None),
        P(("req", "cache"), None),
        P(("req", "cache"), None),
        P(("req", "cache"), None),
        P(("req", "cache"), None),
        P(("req", "cache"), None),
        P(("req", "cache"), None),
        P(),
        P(),
        P(),
        P(),
    )
    out_specs = (P(("req", "cache"), None, None, None), P(("req", "cache"), None, None))
    return jax.shard_map(body, mesh=mesh, in_specs=in_specs, out_specs=out_specs, check_vma=False)
```

```python
import jax
import jax.numpy as jnp
from jax import lax
from jax.experimental import pallas as pl
from jax.experimental.pallas import tpu as pltpu
from jax.sharding import PartitionSpec as P

D = 1024
HEADS = 8
HEAD_DIM = 128
HIST = 64
CB = 128
USERS = 16
REQS = 8
ROWS = 512
LIVE = 512
CHUNK = (16, 16, 16, 16)
CHUNKS = len(CHUNK)
FIRST = tuple(sum(CHUNK[:q]) for q in range(CHUNKS))
LAST = CHUNKS - 1
WINDOW = 256
SCALE = HEAD_DIM ** (-0.5)
MESH = pl.DeviceIdType.MESH
F32 = jnp.float32
BF16 = jnp.bfloat16
I32 = jnp.int32

XY = [(2, 2), (0, 2), (2, 0), (1, 1), (3, 1), (3, 3), (1, 3), (1, 2), (2, 1), (3, 2), (2, 3), (3, 0), (1, 0), (0, 1), (0, 3)]
ZK = [(2, 0), (2, 1), (1, 0), (3, 0), (1, 1), (3, 1), (0, 1)]


def in_hbm(array):
    return pltpu.with_memory_space_constraint(array, pltpu.HBM)


def iota(shape, dim):
    return lax.broadcasted_iota(I32, shape, dim)


def silu(x):
    half = 0.5 * x
    return half + half * jnp.tanh(half)


def masked_silu(x, half_scale):
    half = x * half_scale
    return (half + half * jnp.tanh(half)).astype(BF16)


def norm(x):
    mean = jnp.sum(x, axis=-1, keepdims=True) * (1.0 / D)
    centred = x - mean
    spread = jnp.sum(centred * centred, axis=-1, keepdims=True) * (1.0 / D)
    return centred * lax.rsqrt(spread + 1e-06)


def dot(a, b):
    return jnp.dot(a, b, preferred_element_type=F32)


def dot_nt(a, b):
    return lax.dot_general(a, b, (((1,), (1,)), ((), ())), preferred_element_type=F32)


def cols(i, width):
    return pl.ds(pl.multiple_of(i * width, width), width)


def request_bounds(counts):
    lane = iota((1, REQS), 1)
    starts = [jnp.sum(jnp.where(lane < j, counts, 0.0), axis=1, keepdims=True) for j in range(REQS)]
    lengths = [jnp.sum(jnp.where(lane == j, counts, 0.0), axis=1, keepdims=True) for j in range(REQS)]
    return starts, lengths


def exchange_kernel(
    feats_h, len_h, own_h, ids_h, count_h, rown_h, rslot_h, table_h, wqu_h, wkv_h, wout_h,
    kv, emb, query, gate, att, asked, wkv, wout, mask, spread,
    feats, len_v, own_v, ids_v, count_v, rown_v, rslot_v, table, wqu,
    hn, pick0, pick1, pick2, pick3, send0, send1, send2, send3, recv0, recv1, recv2, recv3, slot_out, slot_in, select,
    stage0, stage1, stage2, stage3, back0, back1, back2, back3, kvr, onehot, cn, skv,
    load_sem, ss1, rs1, ss2, rs2, sss, rss,
):
    r = lax.axis_index("req")
    c = lax.axis_index("cache")
    z, k = r // 2, lax.rem(r, 2)
    y, x = c // 4, lax.rem(c, 4)
    pick = [pick0, pick1, pick2, pick3]
    send = [send0, send1, send2, send3]
    recv = [recv0, recv1, recv2, recv3]
    stage = [stage0, stage1, stage2, stage3]
    back = [back0, back1, back2, back3]

    def plane(offset):
        dy, dx = offset
        return lax.rem(y + dy, 4) * 4 + lax.rem(x + dx, 4)

    def column(offset):
        dz, dk = offset
        return lax.rem(z + dz, 4) * 2 + lax.rem(k + dk, 2)

    pairs = [
        (feats_h, feats), (len_h, len_v), (own_h, own_v), (count_h, count_v), (ids_h, ids_v), (rown_h, rown_v), (rslot_h, rslot_v),
        (table_h, table), (wqu_h, wqu), (wkv_h, wkv), (wout_h, wout),
    ]
    loads = [pltpu.make_async_copy(src, dst, load_sem.at[i]) for i, (src, dst) in enumerate(pairs)]
    for i in (1, 2, 0):
        loads[i].start()

    barrier = pltpu.get_barrier_semaphore()
    for offset in XY:
        pl.semaphore_signal(barrier, inc=1, device_id=(r, plane(offset)), device_id_type=MESH)
    for offset in ZK:
        pl.semaphore_signal(barrier, inc=1, device_id=(column(offset), c), device_id_type=MESH)

    loads[1].wait()
    loads[2].wait()
    lengths = len_v[...].astype(F32)
    owner = own_v[...]
    lane_j = iota((USERS, USERS), 1)
    mine = owner == iota((USERS, USERS), 0)
    order = jnp.sum(jnp.where(mine, lane_j.astype(F32), 0.0), axis=1, keepdims=True)
    length_of = jnp.sum(jnp.where(mine, lengths, 0.0), axis=1, keepdims=True)
    start_of = jnp.sum(jnp.where(lane_j.astype(F32) < order, lengths, 0.0), axis=1, keepdims=True)

    def build_pick(q):
        n = CHUNK[q]
        row = iota((n, ROWS), 1).astype(F32)
        step = iota((n, ROWS), 0).astype(F32) + float(FIRST[q])
        for o in range(USERS):
            place = row - start_of[o : o + 1, :]
            hit = jnp.logical_and(place == step, place < length_of[o : o + 1, :])
            pick[q][o * n : (o + 1) * n, :] = jnp.where(hit, 1.0, 0.0).astype(BF16)

    def slot_copy(i):
        to = column(ZK[i])
        return pltpu.make_async_remote_copy(
            src_ref=slot_out.at[to], dst_ref=slot_in.at[r], send_sem=sss.at[i], recv_sem=rss.at[i],
            device_id=(to, c), device_id_type=MESH,
        )

    def plane_copy(q, i):
        to = plane(XY[i])
        return pltpu.make_async_remote_copy(
            src_ref=send[q].at[cols(to, CHUNK[q]), :], dst_ref=recv[q].at[cols(c, CHUNK[q]), :],
            send_sem=ss1.at[q, i], recv_sem=rs1.at[q, i], device_id=(r, to), device_id_type=MESH,
        )

    def column_copy(q, i):
        to = column(ZK[i])
        return pltpu.make_async_remote_copy(
            src_ref=stage[q].at[cols(to, CHUNK[q]), :], dst_ref=back[q].at[cols(r, CHUNK[q]), :],
            send_sem=ss2.at[q, i], recv_sem=rs2.at[q, i], device_id=(to, c), device_id_type=MESH,
        )

    loads[0].wait()
    for i in range(ROWS // 64):
        rows = slice(i * 64, (i + 1) * 64)
        hn[rows, :] = norm(feats[rows, :].astype(F32)).astype(BF16)
    for q in range(CHUNKS):
        build_pick(q)
        send[q][...] = dot(pick[q][...], hn[...]).astype(BF16)
        if q == 0:
            pl.semaphore_wait(barrier, len(XY) + len(ZK))
        for i in range(len(XY)):
            plane_copy(q, i).start()
        if q == 0:
            for i in range(3, len(loads)):
                loads[i].start()
        own_rows = cols(c, CHUNK[q])
        recv[q][own_rows, :] = send[q][own_rows, :]

    for i in (3, 4, 5, 6):
        loads[i].wait()
    req_owner = rown_v[...]
    req_slot = rslot_v[...]
    for o in range(REQS):
        wanted = jnp.sum(jnp.where(req_owner == o, req_slot.astype(F32), 0.0), axis=1, keepdims=True)
        slot_out[o] = jnp.broadcast_to(wanted, (8, 128)).astype(I32)
    for i in range(len(ZK)):
        slot_copy(i).start()
    slot_in[r] = slot_out[r]

    starts, counts = request_bounds(count_v[...].astype(F32))
    packed = iota((LIVE, CB), 0).astype(F32)
    lane = iota((LIVE, CB), 1).astype(F32)
    id_sum = jnp.zeros((LIVE, CB), F32)
    owner_sum = jnp.zeros((LIVE, CB), F32)
    req_owner_f = req_owner.astype(F32)
    for j in range(REQS):
        place = packed - starts[j]
        hit = jnp.logical_and(place == lane, lane < counts[j])
        id_sum = id_sum + jnp.where(hit, ids_v[0:1, j * CB : (j + 1) * CB].astype(F32), 0.0)
        inside = jnp.logical_and(place >= 0.0, place < counts[j])
        owner_sum = owner_sum + jnp.where(inside, req_owner_f[:, j : j + 1], 0.0)
    mask[...] = jnp.where(owner_sum == (iota((LIVE, CB), 1) // CHUNK[1]).astype(F32), 0.5 * SCALE, 0.0)
    ids = jnp.sum(id_sum, axis=1, keepdims=True)
    for n in range(D // 128):
        word = (iota((LIVE, 128), 1) + n * 128).astype(F32)
        onehot[:, n * 128 : (n + 1) * 128] = jnp.where(ids == word, 1.0, 0.0).astype(BF16)

    loads[7].wait()
    emb[...] = dot(onehot[...], table[...]).astype(BF16)
    for i in range(LIVE // 64):
        rows = slice(i * 64, (i + 1) * 64)
        cn[rows, :] = norm(emb[rows, :].astype(F32)).astype(BF16)
    loads[8].wait()
    query[...] = silu(dot(cn[...], wqu[:, :D])).astype(BF16)
    gate[...] = silu(dot(cn[...], wqu[:, D:])).astype(BF16)
    loads[9].wait()
    skv[...] = silu(dot(cn[...], wkv[...])).astype(BF16)
    for h in range(HEADS):
        head = slice(h * HEAD_DIM, (h + 1) * HEAD_DIM)
        value = slice(D + h * HEAD_DIM, D + (h + 1) * HEAD_DIM)
        product = query[:, head].astype(F32) * skv[:, head].astype(F32)
        weight = silu(jnp.sum(product, axis=1, keepdims=True) * SCALE)
        att[:, head] = weight * skv[:, value].astype(F32)

    slot = iota((CB, WINDOW), 0).astype(F32)
    shifted = iota((CB, WINDOW), 1).astype(F32) - slot
    for j in range(REQS):
        base = jnp.minimum(jnp.floor(starts[j] * (1.0 / 16.0)) * 16.0, float(LIVE - WINDOW))
        hit = jnp.logical_and(shifted == starts[j] - base, slot < counts[j])
        spread[j * CB : (j + 1) * CB, :] = jnp.where(hit, 1.0, 0.0).astype(BF16)

    for i in range(len(ZK)):
        slot_copy(i).wait_recv()
    n = CHUNK[0]
    lane_row = iota((n, USERS * n), 1).astype(F32)
    step = iota((n, USERS * n), 0).astype(F32)
    for o in range(REQS):
        slot = slot_in[o][0:1, 0:1].astype(F32)
        hit = lane_row == slot * float(n) + step
        select[o * n : (o + 1) * n, :] = jnp.where(hit, 1.0, 0.0).astype(BF16)

    def attend_chunk(q):
        for i in range(len(ZK)):
            column_copy(q, i).wait_recv()
        keys = slice(0, REQS * CHUNK[q])
        kvr[keys, :] = silu(dot(back[q][...], wkv[...])).astype(BF16)
        for h in range(HEADS):
            head = slice(h * HEAD_DIM, (h + 1) * HEAD_DIM)
            value = slice(D + h * HEAD_DIM, D + (h + 1) * HEAD_DIM)
            weight = masked_silu(dot_nt(query[:, head], kvr[keys, head]), mask[...])
            att[:, head] += dot(weight, kvr[keys, value])

    for q in range(CHUNKS):
        n = CHUNK[q]
        for i in range(len(XY)):
            plane_copy(q, i).wait_recv()
        stage[q][...] = dot(select[...], recv[q][...]).astype(BF16)
        for i in range(len(ZK)):
            column_copy(q, i).start()
        own_rows = cols(r, n)
        back[q][own_rows, :] = stage[q][own_rows, :]
        block = silu(dot(recv[q][...], wkv[...])).astype(BF16)
        kv[:, FIRST[q] : FIRST[q] + n, :] = block.reshape(USERS, n, 2 * D)
        if q > 0:
            attend_chunk(q - 1)

    for i in range(len(ZK)):
        slot_copy(i).wait_send()
    for q in range(CHUNKS):
        for i in range(len(XY)):
            plane_copy(q, i).wait_send()
        for i in range(len(ZK)):
            column_copy(q, i).wait_send()
    loads[10].wait()
    for i in range(len(ZK)):
        column_copy(LAST, i).wait_recv()
    asked[...] = back[LAST][...]


def exchange(feats, lens, owners, ids, counts, req_owner, req_slot, table, w_qu, w_kv, w_out):
    any_spec = pl.BlockSpec(memory_space=pl.ANY)
    vmem = pltpu.VMEM
    sems = pltpu.SemaphoreType.DMA
    outs = (
        vmem((USERS, HIST, 2 * D), BF16), vmem((LIVE, D), BF16), vmem((LIVE, D), BF16), vmem((LIVE, D), BF16),
        vmem((LIVE, D), F32), vmem((REQS * CHUNK[LAST], D), BF16), vmem((D, 2 * D), BF16), vmem((D, D), BF16),
        vmem((LIVE, REQS * CHUNK[LAST]), F32), vmem((REQS * CB, WINDOW), BF16),
    )
    return pl.pallas_call(
        exchange_kernel,
        out_shape=outs,
        in_specs=[any_spec] * 11,
        out_specs=(pl.BlockSpec(memory_space=vmem),) * len(outs),
        scratch_shapes=[
            vmem((ROWS, D), BF16),
            vmem((1, USERS), I32), vmem((1, USERS), I32), vmem((1, REQS * CB), I32), vmem((1, REQS), I32),
            vmem((1, REQS), I32), vmem((1, REQS), I32),
            vmem((D, D), BF16), vmem((D, 2 * D), BF16),
            vmem((ROWS, D), BF16),
        ]
        + [vmem((USERS * n, ROWS), BF16) for n in CHUNK]
        + [vmem((USERS * n, D), BF16) for n in CHUNK]
        + [vmem((USERS * n, D), BF16) for n in CHUNK]
        + [vmem((REQS, 8, 128), I32), vmem((REQS, 8, 128), I32)]
        + [vmem((REQS * n, USERS * n), BF16) for n in CHUNK[:1]]
        + [vmem((REQS * n, D), BF16) for n in CHUNK]
        + [vmem((REQS * n, D), BF16) for n in CHUNK]
        + [
            vmem((REQS * max(CHUNK), 2 * D), BF16),
            vmem((LIVE, D), BF16), vmem((LIVE, D), BF16), vmem((LIVE, 2 * D), BF16),
            sems((11,)),
            sems((CHUNKS, len(XY))), sems((CHUNKS, len(XY))),
            sems((CHUNKS, len(ZK))), sems((CHUNKS, len(ZK))),
            sems((len(ZK),)), sems((len(ZK),)),
        ],
        compiler_params=pltpu.CompilerParams(collective_id=0, has_side_effects=True, vmem_limit_bytes=40 << 20),
        cost_estimate=pl.CostEstimate(flops=13 << 30, bytes_accessed=20 << 20, transcendentals=8 << 20),
        name="exchange",
    )(feats, lens, owners, ids, counts, req_owner, req_slot, table, w_qu, w_kv, w_out)


def output_kernel(
    cache_in, emb, query, gate, att, asked, wkv, wout, mask, spread, count_h,
    cache_out, cand_h,
    count_s, mixed, gated, res, out,
    sem, cache_sem, out_sem,
):
    load = pltpu.make_async_copy(count_h, count_s, sem)
    load.start()
    moves = [
        pltpu.make_async_copy(cache_in.at[pl.ds(i * 4, 4)], cache_out.at[pl.ds(i * 4, 4)], cache_sem.at[i]) for i in range(4)
    ]
    for copy in moves:
        copy.start()

    block = silu(dot(asked[...], wkv[...])).astype(BF16)
    total = jnp.zeros((LIVE, HEAD_DIM), F32)
    squares = jnp.zeros((LIVE, HEAD_DIM), F32)
    for h in range(HEADS):
        head = slice(h * HEAD_DIM, (h + 1) * HEAD_DIM)
        value = slice(D + h * HEAD_DIM, D + (h + 1) * HEAD_DIM)
        weight = masked_silu(dot_nt(query[:, head], block[:, head]), mask[...])
        part = att[:, head] + dot(weight, block[:, value])
        mixed[:, head] = part
        total = total + part
        squares = squares + part * part
    mean = jnp.sum(total, axis=1, keepdims=True) * (1.0 / D)
    spread_of = jnp.sum(squares, axis=1, keepdims=True) * (1.0 / D) - mean * mean
    scale = lax.rsqrt(jnp.maximum(spread_of, 0.0) + 1e-06)
    for i in range(LIVE // 64):
        rows = slice(i * 64, (i + 1) * 64)
        gated[rows, :] = ((mixed[rows, :] - mean[rows, :]) * (scale[rows, :] * gate[rows, :].astype(F32))).astype(BF16)
    res[...] = (dot(gated[...], wout[...]) + emb[...].astype(F32)).astype(BF16)

    def out_copy(j):
        rows = pl.ds(j * CB, CB)
        return pltpu.make_async_copy(out.at[rows], cand_h.at[rows], out_sem.at[j])

    load.wait()
    start = jnp.int32(0)
    for j in range(REQS):
        base = jnp.minimum((start // 16) * 16, LIVE - WINDOW)
        window = pl.ds(pl.multiple_of(base, 16), WINDOW)
        out[j * CB : (j + 1) * CB, :] = dot(spread[j * CB : (j + 1) * CB, :], res[window, :]).astype(BF16)
        out_copy(j).start()
        start = start + count_s[0, j]
    for j in range(REQS):
        out_copy(j).wait()
    for copy in moves:
        copy.wait()


def output(cache, emb, query, gate, att, asked, w_kv, w_out, mask, spread, counts):
    any_spec = pl.BlockSpec(memory_space=pl.ANY)
    vmem = pltpu.VMEM
    return pl.pallas_call(
        output_kernel,
        out_shape=(
            jax.ShapeDtypeStruct((USERS, HIST, 2 * D), BF16),
            jax.ShapeDtypeStruct((REQS * CB, D), BF16),
        ),
        in_specs=[pl.BlockSpec(memory_space=vmem)] * 10 + [any_spec],
        out_specs=(any_spec,) * 2,
        scratch_shapes=[
            pltpu.SMEM((1, REQS), I32),
            vmem((LIVE, D), F32), vmem((LIVE, D), BF16), vmem((LIVE, D), BF16), vmem((REQS * CB, D), BF16),
            pltpu.SemaphoreType.DMA, pltpu.SemaphoreType.DMA((4,)), pltpu.SemaphoreType.DMA((REQS,)),
        ],
        compiler_params=pltpu.CompilerParams(vmem_limit_bytes=24 << 20),
        cost_estimate=pl.CostEstimate(flops=3 << 30, bytes_accessed=16 << 20, transcendentals=0),
        name="output",
    )(cache, emb, query, gate, att, asked, w_kv, w_out, mask, spread, in_hbm(counts))


def body(event_feats, hist_len, user_owner, cand_ids, cand_count, req_owner, req_slot, table, w_qu, w_kv, w_out):
    held = exchange(
        *(in_hbm(a) for a in (event_feats[0], hist_len, user_owner, cand_ids, cand_count, req_owner, req_slot, table, w_qu, w_kv, w_out))
    )
    cache, cand_out = output(*held, cand_count)
    return (cache[None], cand_out[None])


def solution(mesh):
    in_specs = (
        P(("req", "cache"), None, None),
        P(("req", "cache"), None),
        P(("req", "cache"), None),
        P(("req", "cache"), None),
        P(("req", "cache"), None),
        P(("req", "cache"), None),
        P(("req", "cache"), None),
        P(),
        P(),
        P(),
        P(),
    )
    out_specs = (P(("req", "cache"), None, None, None), P(("req", "cache"), None, None))
    return jax.shard_map(body, mesh=mesh, in_specs=in_specs, out_specs=out_specs, check_vma=False)
```

```python
import jax
import jax.numpy as jnp
from jax import lax
from jax.experimental import pallas as pl
from jax.experimental.pallas import tpu as pltpu
from jax.sharding import PartitionSpec as P

D = 1024
HEADS = 8
HEAD_DIM = 128
HIST = 64
CB = 128
USERS = 16
REQS = 8
ROWS = 512
LIVE = 512
CHUNK = (16, 16, 16, 16)
CHUNKS = len(CHUNK)
FIRST = tuple(sum(CHUNK[:q]) for q in range(CHUNKS))
LAST = CHUNKS - 1
WINDOW = 256
SCALE = HEAD_DIM ** (-0.5)
MESH = pl.DeviceIdType.MESH
F32 = jnp.float32
BF16 = jnp.bfloat16
I32 = jnp.int32

XY = [(2, 2), (0, 2), (2, 0), (1, 1), (3, 1), (3, 3), (1, 3), (1, 2), (2, 1), (3, 2), (2, 3), (3, 0), (1, 0), (0, 1), (0, 3)]
ZK = [(2, 0), (2, 1), (1, 0), (3, 0), (1, 1), (3, 1), (0, 1)]


def in_hbm(array):
    return pltpu.with_memory_space_constraint(array, pltpu.HBM)


def iota(shape, dim):
    return lax.broadcasted_iota(I32, shape, dim)


def silu(x):
    half = 0.5 * x
    return half + half * jnp.tanh(half)


def masked_silu(x, half_scale):
    half = x * half_scale
    return (half + half * jnp.tanh(half)).astype(BF16)


def norm(x):
    mean = jnp.sum(x, axis=-1, keepdims=True) * (1.0 / D)
    centred = x - mean
    spread = jnp.sum(centred * centred, axis=-1, keepdims=True) * (1.0 / D)
    return centred * lax.rsqrt(spread + 1e-06)


def dot(a, b):
    return jnp.dot(a, b, preferred_element_type=F32)


def dot_nt(a, b):
    return lax.dot_general(a, b, (((1,), (1,)), ((), ())), preferred_element_type=F32)


def cols(i, width):
    return pl.ds(pl.multiple_of(i * width, width), width)


def request_bounds(counts):
    lane = iota((1, REQS), 1)
    starts = [jnp.sum(jnp.where(lane < j, counts, 0.0), axis=1, keepdims=True) for j in range(REQS)]
    lengths = [jnp.sum(jnp.where(lane == j, counts, 0.0), axis=1, keepdims=True) for j in range(REQS)]
    return starts, lengths


def exchange_kernel(
    feats_h, len_h, own_h, ids_h, count_h, rown_h, rslot_h, table_h, wqu_h, wkv_h, wout_h,
    kv, emb, query, gate, att, asked, wkv, wout, mask, spread,
    feats, len_v, own_v, ids_v, count_v, rown_v, rslot_v, table, wqu,
    hn, pick0, pick1, pick2, pick3, send0, send1, send2, send3, recv0, recv1, recv2, recv3, slot_out, slot_in, select,
    stage0, stage1, stage2, stage3, back0, back1, back2, back3, kvr, onehot, cn, skv,
    load_sem, ss1, rs1, ss2, rs2, sss, rss,
):
    r = lax.axis_index("req")
    c = lax.axis_index("cache")
    z, k = r // 2, lax.rem(r, 2)
    y, x = c // 4, lax.rem(c, 4)
    pick = [pick0, pick1, pick2, pick3]
    send = [send0, send1, send2, send3]
    recv = [recv0, recv1, recv2, recv3]
    stage = [stage0, stage1, stage2, stage3]
    back = [back0, back1, back2, back3]

    def plane(offset):
        dy, dx = offset
        return lax.rem(y + dy, 4) * 4 + lax.rem(x + dx, 4)

    def column(offset):
        dz, dk = offset
        return lax.rem(z + dz, 4) * 2 + lax.rem(k + dk, 2)

    pairs = [
        (feats_h, feats), (len_h, len_v), (own_h, own_v), (count_h, count_v), (ids_h, ids_v), (rown_h, rown_v), (rslot_h, rslot_v),
        (table_h, table), (wqu_h, wqu), (wkv_h, wkv), (wout_h, wout),
    ]
    loads = [pltpu.make_async_copy(src, dst, load_sem.at[i]) for i, (src, dst) in enumerate(pairs)]
    for i in (1, 2, 0):
        loads[i].start()

    barrier = pltpu.get_barrier_semaphore()
    for offset in XY:
        pl.semaphore_signal(barrier, inc=1, device_id=(r, plane(offset)), device_id_type=MESH)
    for offset in ZK:
        pl.semaphore_signal(barrier, inc=1, device_id=(column(offset), c), device_id_type=MESH)

    loads[1].wait()
    loads[2].wait()
    lengths = len_v[...].astype(F32)
    owner = own_v[...]
    lane_j = iota((USERS, USERS), 1)
    mine = owner == iota((USERS, USERS), 0)
    order = jnp.sum(jnp.where(mine, lane_j.astype(F32), 0.0), axis=1, keepdims=True)
    length_of = jnp.sum(jnp.where(mine, lengths, 0.0), axis=1, keepdims=True)
    start_of = jnp.sum(jnp.where(lane_j.astype(F32) < order, lengths, 0.0), axis=1, keepdims=True)

    def build_pick(q):
        n = CHUNK[q]
        row = iota((n, ROWS), 1).astype(F32)
        step = iota((n, ROWS), 0).astype(F32) + float(FIRST[q])
        for o in range(USERS):
            place = row - start_of[o : o + 1, :]
            hit = jnp.logical_and(place == step, place < length_of[o : o + 1, :])
            pick[q][o * n : (o + 1) * n, :] = jnp.where(hit, 1.0, 0.0).astype(BF16)

    def slot_copy(i):
        to = column(ZK[i])
        return pltpu.make_async_remote_copy(
            src_ref=slot_out.at[to], dst_ref=slot_in.at[r], send_sem=sss.at[i], recv_sem=rss.at[i],
            device_id=(to, c), device_id_type=MESH,
        )

    def plane_copy(q, i):
        to = plane(XY[i])
        return pltpu.make_async_remote_copy(
            src_ref=send[q].at[cols(to, CHUNK[q]), :], dst_ref=recv[q].at[cols(c, CHUNK[q]), :],
            send_sem=ss1.at[q, i], recv_sem=rs1.at[q, i], device_id=(r, to), device_id_type=MESH,
        )

    def column_copy(q, i):
        to = column(ZK[i])
        return pltpu.make_async_remote_copy(
            src_ref=stage[q].at[cols(to, CHUNK[q]), :], dst_ref=back[q].at[cols(r, CHUNK[q]), :],
            send_sem=ss2.at[q, i], recv_sem=rs2.at[q, i], device_id=(to, c), device_id_type=MESH,
        )

    loads[0].wait()
    for i in range(ROWS // 64):
        rows = slice(i * 64, (i + 1) * 64)
        hn[rows, :] = norm(feats[rows, :].astype(F32)).astype(BF16)
    for q in range(CHUNKS):
        build_pick(q)
        send[q][...] = dot(pick[q][...], hn[...]).astype(BF16)
        if q == 0:
            pl.semaphore_wait(barrier, len(XY) + len(ZK))
        for i in range(len(XY)):
            plane_copy(q, i).start()
        if q == 0:
            for i in range(3, len(loads)):
                loads[i].start()
        own_rows = cols(c, CHUNK[q])
        recv[q][own_rows, :] = send[q][own_rows, :]

    for i in (3, 4, 5, 6):
        loads[i].wait()
    req_owner = rown_v[...]
    req_slot = rslot_v[...]
    for o in range(REQS):
        wanted = jnp.sum(jnp.where(req_owner == o, req_slot.astype(F32), 0.0), axis=1, keepdims=True)
        slot_out[o] = jnp.broadcast_to(wanted, (8, 128)).astype(I32)
    for i in range(len(ZK)):
        slot_copy(i).start()
    slot_in[r] = slot_out[r]

    starts, counts = request_bounds(count_v[...].astype(F32))
    packed = iota((LIVE, CB), 0).astype(F32)
    lane = iota((LIVE, CB), 1).astype(F32)
    id_sum = jnp.zeros((LIVE, CB), F32)
    owner_sum = jnp.zeros((LIVE, CB), F32)
    req_owner_f = req_owner.astype(F32)
    for j in range(REQS):
        place = packed - starts[j]
        hit = jnp.logical_and(place == lane, lane < counts[j])
        id_sum = id_sum + jnp.where(hit, ids_v[0:1, j * CB : (j + 1) * CB].astype(F32), 0.0)
        inside = jnp.logical_and(place >= 0.0, place < counts[j])
        owner_sum = owner_sum + jnp.where(inside, req_owner_f[:, j : j + 1], 0.0)
    mask[...] = jnp.where(owner_sum == (iota((LIVE, CB), 1) // CHUNK[1]).astype(F32), 0.5 * SCALE, 0.0)
    ids = jnp.sum(id_sum, axis=1, keepdims=True)
    for n in range(D // 128):
        word = (iota((LIVE, 128), 1) + n * 128).astype(F32)
        onehot[:, n * 128 : (n + 1) * 128] = jnp.where(ids == word, 1.0, 0.0).astype(BF16)

    loads[7].wait()
    emb[...] = dot(onehot[...], table[...]).astype(BF16)
    for i in range(LIVE // 64):
        rows = slice(i * 64, (i + 1) * 64)
        cn[rows, :] = norm(emb[rows, :].astype(F32)).astype(BF16)
    loads[8].wait()
    query[...] = silu(dot(cn[...], wqu[:, :D])).astype(BF16)
    gate[...] = silu(dot(cn[...], wqu[:, D:])).astype(BF16)
    loads[9].wait()
    skv[...] = silu(dot(cn[...], wkv[...])).astype(BF16)
    for h in range(HEADS):
        head = slice(h * HEAD_DIM, (h + 1) * HEAD_DIM)
        value = slice(D + h * HEAD_DIM, D + (h + 1) * HEAD_DIM)
        product = query[:, head].astype(F32) * skv[:, head].astype(F32)
        weight = silu(jnp.sum(product, axis=1, keepdims=True) * SCALE)
        att[:, head] = weight * skv[:, value].astype(F32)

    slot = iota((CB, WINDOW), 0).astype(F32)
    shifted = iota((CB, WINDOW), 1).astype(F32) - slot
    for j in range(REQS):
        base = jnp.minimum(jnp.floor(starts[j] * (1.0 / 16.0)) * 16.0, float(LIVE - WINDOW))
        hit = jnp.logical_and(shifted == starts[j] - base, slot < counts[j])
        spread[j * CB : (j + 1) * CB, :] = jnp.where(hit, 1.0, 0.0).astype(BF16)

    for i in range(len(ZK)):
        slot_copy(i).wait_recv()
    n = CHUNK[0]
    lane_row = iota((n, USERS * n), 1).astype(F32)
    step = iota((n, USERS * n), 0).astype(F32)
    for o in range(REQS):
        slot = slot_in[o][0:1, 0:1].astype(F32)
        hit = lane_row == slot * float(n) + step
        select[o * n : (o + 1) * n, :] = jnp.where(hit, 1.0, 0.0).astype(BF16)

    def attend_chunk(q):
        for i in range(len(ZK)):
            column_copy(q, i).wait_recv()
        keys = slice(0, REQS * CHUNK[q])
        kvr[keys, :] = silu(dot(back[q][...], wkv[...])).astype(BF16)
        for h in range(HEADS):
            head = slice(h * HEAD_DIM, (h + 1) * HEAD_DIM)
            value = slice(D + h * HEAD_DIM, D + (h + 1) * HEAD_DIM)
            weight = masked_silu(dot_nt(query[:, head], kvr[keys, head]), mask[...])
            att[:, head] += dot(weight, kvr[keys, value])

    for q in range(CHUNKS):
        n = CHUNK[q]
        for i in range(len(XY)):
            plane_copy(q, i).wait_recv()
        stage[q][...] = dot(select[...], recv[q][...]).astype(BF16)
        for i in range(len(ZK)):
            column_copy(q, i).start()
        own_rows = cols(r, n)
        back[q][own_rows, :] = stage[q][own_rows, :]
        block = silu(dot(recv[q][...], wkv[...])).astype(BF16)
        kv[:, FIRST[q] : FIRST[q] + n, :] = block.reshape(USERS, n, 2 * D)
        if q > 0:
            attend_chunk(q - 1)

    for i in range(len(ZK)):
        slot_copy(i).wait_send()
    for q in range(CHUNKS):
        for i in range(len(XY)):
            plane_copy(q, i).wait_send()
        for i in range(len(ZK)):
            column_copy(q, i).wait_send()
    loads[10].wait()
    for i in range(len(ZK)):
        column_copy(LAST, i).wait_recv()
    asked[...] = back[LAST][...]


def exchange(feats, lens, owners, ids, counts, req_owner, req_slot, table, w_qu, w_kv, w_out):
    any_spec = pl.BlockSpec(memory_space=pl.ANY)
    vmem = pltpu.VMEM
    sems = pltpu.SemaphoreType.DMA
    outs = (
        vmem((USERS, HIST, 2 * D), BF16), vmem((LIVE, D), BF16), vmem((LIVE, D), BF16), vmem((LIVE, D), BF16),
        vmem((LIVE, D), F32), vmem((REQS * CHUNK[LAST], D), BF16), vmem((D, 2 * D), BF16), vmem((D, D), BF16),
        vmem((LIVE, REQS * CHUNK[LAST]), F32), vmem((REQS * CB, WINDOW), BF16),
    )
    return pl.pallas_call(
        exchange_kernel,
        out_shape=outs,
        in_specs=[any_spec] * 11,
        out_specs=(pl.BlockSpec(memory_space=vmem),) * len(outs),
        scratch_shapes=[
            vmem((ROWS, D), BF16),
            vmem((1, USERS), I32), vmem((1, USERS), I32), vmem((1, REQS * CB), I32), vmem((1, REQS), I32),
            vmem((1, REQS), I32), vmem((1, REQS), I32),
            vmem((D, D), BF16), vmem((D, 2 * D), BF16),
            vmem((ROWS, D), BF16),
        ]
        + [vmem((USERS * n, ROWS), BF16) for n in CHUNK]
        + [vmem((USERS * n, D), BF16) for n in CHUNK]
        + [vmem((USERS * n, D), BF16) for n in CHUNK]
        + [vmem((REQS, 8, 128), I32), vmem((REQS, 8, 128), I32)]
        + [vmem((REQS * n, USERS * n), BF16) for n in CHUNK[:1]]
        + [vmem((REQS * n, D), BF16) for n in CHUNK]
        + [vmem((REQS * n, D), BF16) for n in CHUNK]
        + [
            vmem((REQS * max(CHUNK), 2 * D), BF16),
            vmem((LIVE, D), BF16), vmem((LIVE, D), BF16), vmem((LIVE, 2 * D), BF16),
            sems((11,)),
            sems((CHUNKS, len(XY))), sems((CHUNKS, len(XY))),
            sems((CHUNKS, len(ZK))), sems((CHUNKS, len(ZK))),
            sems((len(ZK),)), sems((len(ZK),)),
        ],
        compiler_params=pltpu.CompilerParams(collective_id=0, has_side_effects=True, vmem_limit_bytes=40 << 20),
        cost_estimate=pl.CostEstimate(flops=13 << 30, bytes_accessed=20 << 20, transcendentals=8 << 20),
        name="exchange",
    )(feats, lens, owners, ids, counts, req_owner, req_slot, table, w_qu, w_kv, w_out)


def output_kernel(
    cache_in, emb, query, gate, att, asked, wkv, wout, mask, spread, count_h,
    cache_out, cand_h,
    count_s, mixed, gated, res, out,
    sem, cache_sem, out_sem,
):
    load = pltpu.make_async_copy(count_h, count_s, sem)
    load.start()
    moves = [
        pltpu.make_async_copy(cache_in.at[pl.ds(i * 4, 4)], cache_out.at[pl.ds(i * 4, 4)], cache_sem.at[i]) for i in range(4)
    ]
    for copy in moves:
        copy.start()

    block = silu(dot(asked[...], wkv[...])).astype(BF16)
    total = jnp.zeros((LIVE, HEAD_DIM), F32)
    squares = jnp.zeros((LIVE, HEAD_DIM), F32)
    for h in range(HEADS):
        head = slice(h * HEAD_DIM, (h + 1) * HEAD_DIM)
        value = slice(D + h * HEAD_DIM, D + (h + 1) * HEAD_DIM)
        weight = masked_silu(dot_nt(query[:, head], block[:, head]), mask[...])
        part = att[:, head] + dot(weight, block[:, value])
        mixed[:, head] = part
        total = total + part
        squares = squares + part * part
    mean = jnp.sum(total, axis=1, keepdims=True) * (1.0 / D)
    spread_of = jnp.sum(squares, axis=1, keepdims=True) * (1.0 / D) - mean * mean
    scale = lax.rsqrt(jnp.maximum(spread_of, 0.0) + 1e-06)
    for half in range(2):
        part_rows = slice(half * LIVE // 2, (half + 1) * LIVE // 2)
        for i in range(LIVE // 128):
            first = half * LIVE // 2 + i * 64
            rows = slice(first, first + 64)
            gated[rows, :] = ((mixed[rows, :] - mean[rows, :]) * (scale[rows, :] * gate[rows, :].astype(F32))).astype(BF16)
        res[part_rows, :] = (dot(gated[part_rows, :], wout[...]) + emb[part_rows, :].astype(F32)).astype(BF16)

    def out_copy(j):
        rows = pl.ds(j * CB, CB)
        return pltpu.make_async_copy(out.at[rows], cand_h.at[rows], out_sem.at[j])

    load.wait()
    start = jnp.int32(0)
    for j in range(REQS):
        base = jnp.minimum((start // 16) * 16, LIVE - WINDOW)
        window = pl.ds(pl.multiple_of(base, 16), WINDOW)
        out[j * CB : (j + 1) * CB, :] = dot(spread[j * CB : (j + 1) * CB, :], res[window, :]).astype(BF16)
        out_copy(j).start()
        start = start + count_s[0, j]
    for j in range(REQS):
        out_copy(j).wait()
    for copy in moves:
        copy.wait()


def output(cache, emb, query, gate, att, asked, w_kv, w_out, mask, spread, counts):
    any_spec = pl.BlockSpec(memory_space=pl.ANY)
    vmem = pltpu.VMEM
    return pl.pallas_call(
        output_kernel,
        out_shape=(
            jax.ShapeDtypeStruct((USERS, HIST, 2 * D), BF16),
            jax.ShapeDtypeStruct((REQS * CB, D), BF16),
        ),
        in_specs=[pl.BlockSpec(memory_space=vmem)] * 10 + [any_spec],
        out_specs=(any_spec,) * 2,
        scratch_shapes=[
            pltpu.SMEM((1, REQS), I32),
            vmem((LIVE, D), F32), vmem((LIVE, D), BF16), vmem((LIVE, D), BF16), vmem((REQS * CB, D), BF16),
            pltpu.SemaphoreType.DMA, pltpu.SemaphoreType.DMA((4,)), pltpu.SemaphoreType.DMA((REQS,)),
        ],
        compiler_params=pltpu.CompilerParams(vmem_limit_bytes=24 << 20),
        cost_estimate=pl.CostEstimate(flops=3 << 30, bytes_accessed=16 << 20, transcendentals=0),
        name="output",
    )(cache, emb, query, gate, att, asked, w_kv, w_out, mask, spread, in_hbm(counts))


def body(event_feats, hist_len, user_owner, cand_ids, cand_count, req_owner, req_slot, table, w_qu, w_kv, w_out):
    held = exchange(
        *(in_hbm(a) for a in (event_feats[0], hist_len, user_owner, cand_ids, cand_count, req_owner, req_slot, table, w_qu, w_kv, w_out))
    )
    cache, cand_out = output(*held, cand_count)
    return (cache[None], cand_out[None])


def solution(mesh):
    in_specs = (
        P(("req", "cache"), None, None),
        P(("req", "cache"), None),
        P(("req", "cache"), None),
        P(("req", "cache"), None),
        P(("req", "cache"), None),
        P(("req", "cache"), None),
        P(("req", "cache"), None),
        P(),
        P(),
        P(),
        P(),
    )
    out_specs = (P(("req", "cache"), None, None, None), P(("req", "cache"), None, None))
    return jax.shard_map(body, mesh=mesh, in_specs=in_specs, out_specs=out_specs, check_vma=False)
```
